128 devices in a mesh: batch: 4 (over y), tp: 4 (over z), ep: 8 (over x, core).
Axes of the slice: x: 4, y: 4, z: 4, core: 2. Of those that a mesh axis runs over, the one named last changes fastest.
Arguments:
- states: bfloat16 [32, 512, 2048], P(('batch', 'ep')), may hold values from -30 to 30
- input_gain: float32 [2048], replicated, may hold values from 0.1 to 1.9
- query_weight: bfloat16 [2048, 4096], P(None, 'tp'), may hold values from -0.125 to 0.125
- key_weight: bfloat16 [2048, 512], P(None, 'tp'), may hold values from -0.125 to 0.125
- value_weight: bfloat16 [2048, 512], P(None, 'tp'), may hold values from -0.125 to 0.125
- query_gain: float32 [128], replicated, may hold values from 1 to 2.5
- key_gain: float32 [128], replicated, may hold values from 0.4 to 1.6
- output_weight: bfloat16 [4096, 2048], P('tp'), may hold values from -0.09375 to 0.09375
- mixture_gain: float32 [2048], replicated, may hold values from 0.1 to 1.9
- expert_gate: bfloat16 [128, 2048, 768], P(('batch', 'tp', 'ep')), may hold values from -0.125 to 0.125
- expert_up: bfloat16 [128, 2048, 768], P(('batch', 'tp', 'ep')), may hold values from -0.125 to 0.125
- expert_down: bfloat16 [128, 768, 2048], P(('batch', 'tp', 'ep')), may hold values from -0.21875 to 0.21875
- gate_scale: float32 [128, 768], P(('batch', 'tp', 'ep')), may hold values from 0.5 to 2
- up_scale: float32 [128, 768], P(('batch', 'tp', 'ep')), may hold values from 0.5 to 2
- down_scale: float32 [128, 2048], P(('batch', 'tp', 'ep')), may hold values from 0.5 to 2
- expert_index: int32 [32, 512, 8], P(('batch', 'ep'), 'tp'), may hold values from 0 to 127, as said below
- expert_slot: int32 [32, 512, 8], P(('batch', 'ep'), 'tp'), may hold values from 0 to 9, as said below
- route_weight: float32 [32, 512, 8], P(('batch', 'ep'), 'tp'), may hold values from 0.05 to 0.35
Outputs:
- layer_output: bfloat16 [32, 512, 2048], P(('batch', 'ep'), 'tp')
The draws below stay inside these ranges and needn't reach their ends.
Inputs may be any that keep to these rules, and one draw needn't show every extreme that they name: `expert_index`: the 8 experts of a token differ. A pair's positions fall into aligned blocks of 128; within one block no expert is named by more than 10 tokens, in every block some expert is named by exactly 10 tokens, and one expert is named by exactly 10 tokens in every block. `expert_slot`: within one aligned block of 128 positions of a pair, the tokens that name the same expert carry different slots.
All inputs are finite; a program needn't handle non-finite values.
Results may differ from the reference program's by a relative error of at most 0.012.
Values may be sent and summed in bfloat16 or wider, within the bound.
A program may use at most 128 MiB of HBM per device.

```python
import math
import jax
import jax.numpy as jnp
from jax import lax

D = 2048
QH = 32
KVH = 4
HD = 128
FF = 768
TOP = 8
SEQ = 512
EXPERTS = 128
PAIRS = 32
TOK_BLOCK = 128
CAP = 10


def route_tables(key):
    block_count = PAIRS * (SEQ // TOK_BLOCK)
    strand = EXPERTS // TOP
    slot_span = strand * CAP
    key_common, key_local, key_order, key_rows, key_cols = jax.random.split(key, 5)
    common = jax.random.randint(key_common, (1, 1), 0, strand)
    local = jax.random.randint(key_local, (block_count, TOP - 1), 0, strand)
    full_expert = jnp.concatenate([jnp.broadcast_to(common, (block_count, 1)), local], axis=1)
    cells = jnp.arange(slot_span, dtype=jnp.int32)
    noise_bits = jax.random.randint(key_order, (block_count, TOP, slot_span), 0, 1 << 20)
    scores = noise_bits * slot_span + cells
    scores = jnp.where((cells // CAP)[None, None, :] == full_expert[:, :, None], cells - slot_span, scores)
    ordering = jnp.argsort(scores, axis=-1)[..., :TOK_BLOCK]
    row_bits = jax.random.randint(key_rows, (block_count, TOP, TOK_BLOCK), 0, 1 << 20) * TOK_BLOCK + jnp.arange(TOK_BLOCK, dtype=jnp.int32)
    shuffle = jnp.argsort(row_bits, axis=-1)
    picked = jnp.take_along_axis(ordering, shuffle, axis=-1)
    strand_base = (jnp.arange(TOP, dtype=jnp.int32) * strand)[None, :, None]
    experts_chosen = jnp.transpose(strand_base + picked // CAP, (0, 2, 1))
    slots_chosen = jnp.transpose(picked % CAP, (0, 2, 1))
    col_bits = jax.random.randint(key_cols, (block_count, TOK_BLOCK, TOP), 0, 1 << 20) * TOP + jnp.arange(TOP, dtype=jnp.int32)
    column_order = jnp.argsort(col_bits, axis=-1)
    experts_chosen = jnp.take_along_axis(experts_chosen, column_order, axis=-1)
    slots_chosen = jnp.take_along_axis(slots_chosen, column_order, axis=-1)
    return (experts_chosen.reshape(PAIRS, SEQ, TOP).astype(jnp.int32), slots_chosen.reshape(PAIRS, SEQ, TOP).astype(jnp.int32))


def draw_expert_index(key, part):
    experts_chosen, slots_chosen = route_tables(key)
    return experts_chosen


def draw_expert_slot(key, part):
    experts_chosen, slots_chosen = route_tables(key)
    return slots_chosen


def draw_states(key, part):
    key = jax.random.fold_in(key, 7)
    key_base, key_cols, key_rows = jax.random.split(key, 3)
    column_scale = jnp.exp(jax.random.uniform(key_cols, (D,), minval=-1.15, maxval=1.15))
    row_scale = jnp.exp(jax.random.uniform(key_rows, (PAIRS, SEQ, 1), minval=-1.15, maxval=1.15))
    base = jax.random.normal(key_base, (PAIRS, SEQ, D))
    return jnp.clip(0.5 * base * column_scale * row_scale, -30.0, 30.0).astype(jnp.bfloat16)


def steps_of(rng, extent, cuts, least, high):
    loudness = 1.0
    for axis_at, parts in cuts:
        heights = jax.random.uniform(jax.random.fold_in(jax.random.fold_in(rng, 6), axis_at), (parts,), jnp.float32, least / len(cuts), high / len(cuts))
        loudness = loudness * jnp.repeat(jnp.exp(heights), extent[axis_at] // parts).reshape((-1,) + (1,) * (len(extent) - 1 - axis_at))
    return loudness


def gaussian(rng, shape, spread, most, cuts=(), held_as=jnp.bfloat16):
    loudness = steps_of(rng, shape, cuts, -0.22, 0.18) if cuts else 1.0
    array = jax.random.normal(rng, shape, jnp.float32) * spread * loudness
    return jnp.minimum(jnp.maximum(array, -most), most).astype(held_as)


def setup_inputs(seed: int = 0) -> dict:
    streams_of = jax.random.split(jax.random.key(seed), 19)
    return {
        "states": draw_states(jax.random.fold_in(streams_of[18], 71), 0),
        "input_gain": jnp.clip(1.0 + 0.18 * jax.random.normal(streams_of[1], (D,), jnp.float32), 0.1, 1.9),
        "query_weight": gaussian(streams_of[2], (D, QH * HD), D ** -0.5, 0.125, ((1, 4),)),
        "key_weight": gaussian(streams_of[3], (D, KVH * HD), D ** -0.5, 0.125, ((1, 4),)),
        "value_weight": gaussian(streams_of[4], (D, KVH * HD), D ** -0.5, 0.125, ((1, 4),)),
        "query_gain": jnp.clip(jnp.exp(jax.random.uniform(streams_of[5], (HD,), jnp.float32, math.log(1.0), math.log(2.5))), 1.0, 2.5),
        "key_gain": jnp.clip(1.0 + 0.12 * jax.random.normal(streams_of[6], (HD,), jnp.float32), 0.4, 1.6),
        "output_weight": gaussian(streams_of[7], (QH * HD, D), (QH * HD) ** -0.5, 0.09375, ((0, 4),)),
        "mixture_gain": jnp.clip(1.0 + 0.18 * jax.random.normal(streams_of[8], (D,), jnp.float32), 0.1, 1.9),
        "expert_gate": gaussian(streams_of[9], (EXPERTS, D, FF), D ** -0.5, 0.125, ((0, 128),)),
        "expert_up": gaussian(streams_of[10], (EXPERTS, D, FF), D ** -0.5, 0.125, ((0, 128),)),
        "expert_down": gaussian(streams_of[11], (EXPERTS, FF, D), FF ** -0.5, 0.21875, ((0, 128),)),
        "gate_scale": jnp.clip(jnp.exp(math.log(2.0) - 1.3862944 * jax.random.uniform(streams_of[12], (EXPERTS, FF), jnp.float32) ** steps_of(streams_of[12], (EXPERTS, FF), ((0, 128),), -0.2, 0.2)), 0.5, 2.0),
        "up_scale": jnp.clip(jnp.exp(math.log(2.0) - 1.3862944 * jax.random.uniform(streams_of[13], (EXPERTS, FF), jnp.float32) ** steps_of(streams_of[13], (EXPERTS, FF), ((0, 128),), -0.2, 0.2)), 0.5, 2.0),
        "down_scale": jnp.clip(jnp.exp(math.log(2.0) - 1.3862944 * jax.random.uniform(streams_of[14], (EXPERTS, D), jnp.float32) ** steps_of(streams_of[14], (EXPERTS, D), ((0, 128),), -0.2, 0.2)), 0.5, 2.0),
        "expert_index": draw_expert_index(jax.random.fold_in(streams_of[18], 71), 0),
        "expert_slot": draw_expert_slot(jax.random.fold_in(streams_of[18], 71), 0),
        "route_weight": jnp.clip(0.05 + 0.29999999 * jax.random.uniform(streams_of[17], (PAIRS, SEQ, TOP), jnp.float32) ** steps_of(streams_of[17], (PAIRS, SEQ, TOP), ((0, 32), (1, 4)), -0.2, 0.2), 0.05, 0.35),
    }


def rms_scale(values, scaling):
    mean_square = lax.optimization_barrier(jnp.mean(values * values, axis=-1, keepdims=True))
    return values * lax.rsqrt(mean_square + 1e-06) * scaling

def rotate(values, positions):
    half_dim = values.shape[-1] // 2
    freq_index = jnp.arange(half_dim, dtype=jnp.float32)
    frequency = jnp.exp(-(2.0 * freq_index / values.shape[-1]) * math.log(1000000.0))
    angles = positions[:, None] * frequency[None, :]
    cosine_table = jnp.cos(angles)[:, None, :]
    sine_table = jnp.sin(angles)[:, None, :]
    first_half = values[..., :half_dim]
    second = values[..., half_dim:]
    return jnp.concatenate([first_half * cosine_table - second * sine_table, second * cosine_table + first_half * sine_table], axis=-1)

def attend(pair_states, input_gain, query_weight, key_weight, value_weight, query_gain, key_gain):
    pair_count, length, features = pair_states.shape
    head_size = query_gain.shape[0]
    normed = rms_scale(pair_states.astype(jnp.float32), input_gain).astype(jnp.bfloat16).reshape(pair_count * length, features)
    positions = jnp.arange(length, dtype=jnp.float32)
    queries = jnp.dot(normed, query_weight, preferred_element_type=jnp.float32).reshape(pair_count, length, -1, head_size)
    queries = rotate(rms_scale(queries, query_gain), positions).astype(jnp.bfloat16)
    key_vectors = jnp.dot(normed, key_weight, preferred_element_type=jnp.float32).reshape(pair_count, length, -1, head_size)
    key_vectors = rotate(rms_scale(key_vectors, key_gain), positions).astype(jnp.bfloat16)
    value_vectors = jnp.dot(normed, value_weight, preferred_element_type=jnp.float32).astype(jnp.bfloat16).reshape(pair_count, length, -1, head_size)
    kv_count = key_vectors.shape[2]
    group_size = queries.shape[2] // kv_count
    queries = queries.reshape(pair_count, length, kv_count, group_size, head_size)
    scores = jnp.einsum('pshgd,pthd->phgst', queries.astype(jnp.float32), key_vectors.astype(jnp.float32)) * (1.0 / math.sqrt(head_size))
    weights = jnp.exp(scores)
    probabilities = (weights / lax.optimization_barrier(jnp.sum(weights, axis=-1, keepdims=True))).astype(jnp.bfloat16)
    context = jnp.einsum('phgst,pthd->pshgd', probabilities.astype(jnp.float32), value_vectors.astype(jnp.float32))
    return context.astype(jnp.bfloat16).reshape(pair_count, length, -1)

def feed_forward(token_rows, gate_w, up_w, down_w, gate_s, up_s, down_s):
    gate_part = jnp.dot(token_rows, gate_w, preferred_element_type=jnp.float32) * gate_s
    up_part = jnp.dot(token_rows, up_w, preferred_element_type=jnp.float32) * up_s
    activated = (jax.nn.silu(gate_part) * up_part).astype(jnp.bfloat16)
    return (jnp.dot(activated, down_w, preferred_element_type=jnp.float32) * down_s).astype(jnp.bfloat16)

def reference(states, input_gain, query_weight, key_weight, value_weight, query_gain, key_gain, output_weight, mixture_gain, expert_gate, expert_up, expert_down, gate_scale, up_scale, down_scale, expert_index, expert_slot, route_weight):

    def one_pair(pair_states):
        return attend(pair_states[None], input_gain, query_weight, key_weight, value_weight, query_gain, key_gain)[0]
    context = lax.map(one_pair, states)
    token_total = PAIRS * SEQ
    projected = jnp.dot(context.reshape(token_total, QH * HD), output_weight, preferred_element_type=jnp.float32)
    hidden_state = states.reshape(token_total, D).astype(jnp.float32) + projected
    expert_input = rms_scale(hidden_state, mixture_gain).astype(jnp.bfloat16)
    block_count = PAIRS * (SEQ // TOK_BLOCK)
    token_index = jnp.arange(token_total, dtype=jnp.int32)
    block_index = token_index // TOK_BLOCK
    columns = (block_index[:, None] * CAP + expert_slot.reshape(token_total, TOP).astype(jnp.int32)).reshape(-1)
    chosen = expert_index.reshape(-1).astype(jnp.int32)
    owners = jnp.full((EXPERTS, block_count * CAP), token_total, dtype=jnp.int32).at[chosen, columns].set(jnp.repeat(token_index, TOP))
    shares = jnp.zeros((EXPERTS, block_count * CAP), jnp.float32).at[chosen, columns].set(route_weight.reshape(-1).astype(jnp.float32))
    padded = jnp.concatenate([expert_input, jnp.zeros((1, D), jnp.bfloat16)], axis=0)

    def expert_step(totals, inputs):
        owner_rows, share_rows, gate_w, up_w, down_w, gate_s, up_s, down_s = inputs
        result = feed_forward(padded[owner_rows], gate_w, up_w, down_w, gate_s, up_s, down_s)
        return (totals.at[owner_rows].add(share_rows[:, None] * result.astype(jnp.float32)), None)
    totals, unused = lax.scan(expert_step, jnp.zeros((token_total + 1, D), jnp.float32), (owners, shares, expert_gate, expert_up, expert_down, gate_scale, up_scale, down_scale))
    return (hidden_state + totals[:token_total]).astype(jnp.bfloat16).reshape(PAIRS, SEQ, D)
```

```python
import math

import jax
import jax.numpy as jnp
import numpy as np
from jax import lax
from jax.experimental import pallas as pl
from jax.experimental.pallas import tpu as pltpu
from jax.sharding import PartitionSpec as P


def rms_scale(values, scaling):
    mean_square = jnp.mean(values * values, axis=-1, keepdims=True)
    return values * lax.rsqrt(mean_square + 1e-06) * scaling


def rotate(values, positions):
    half_dim = values.shape[-1] // 2
    freq_index = jnp.arange(half_dim, dtype=jnp.float32)
    frequency = jnp.exp(-(2.0 * freq_index / values.shape[-1]) * math.log(1000000.0))
    angles = positions[:, None] * frequency[None, :]
    cosine_table = jnp.cos(angles)[:, None, :]
    sine_table = jnp.sin(angles)[:, None, :]
    first_half = values[..., :half_dim]
    second = values[..., half_dim:]
    return jnp.concatenate(
        [
            first_half * cosine_table - second * sine_table,
            second * cosine_table + first_half * sine_table,
        ],
        axis=-1,
    )


def attend(pair_states, input_gain, query_weight, key_weight, value_weight, query_gain, key_gain):
    pair_count, length, features = pair_states.shape
    head_size = query_gain.shape[0]
    normed = (
        rms_scale(pair_states.astype(jnp.float32), input_gain)
        .astype(jnp.bfloat16)
        .reshape(pair_count * length, features)
    )
    positions = jnp.arange(length, dtype=jnp.float32)
    queries = jnp.dot(normed, query_weight, preferred_element_type=jnp.float32).reshape(
        pair_count, length, -1, head_size
    )
    queries = rotate(rms_scale(queries, query_gain), positions).astype(jnp.bfloat16)
    key_vectors = jnp.dot(normed, key_weight, preferred_element_type=jnp.float32).reshape(
        pair_count, length, -1, head_size
    )
    key_vectors = rotate(rms_scale(key_vectors, key_gain), positions).astype(jnp.bfloat16)
    value_vectors = (
        jnp.dot(normed, value_weight, preferred_element_type=jnp.float32)
        .astype(jnp.bfloat16)
        .reshape(pair_count, length, -1, head_size)
    )
    kv_count = key_vectors.shape[2]
    group_size = queries.shape[2] // kv_count
    queries = queries.reshape(pair_count, length, kv_count, group_size, head_size)
    scores = jnp.einsum(
        "pshgd,pthd->phgst", queries, key_vectors, preferred_element_type=jnp.float32
    ) * (1.0 / math.sqrt(head_size))
    weights = jnp.exp(scores)
    probabilities = (weights / jnp.sum(weights, axis=-1, keepdims=True)).astype(jnp.bfloat16)
    context = jnp.einsum(
        "phgst,pthd->pshgd", probabilities, value_vectors, preferred_element_type=jnp.float32
    )
    return context.astype(jnp.bfloat16).reshape(pair_count, length, -1)


MESH = pl.DeviceIdType.MESH
CUTS = ((0, 768), (768, 640), (1408, 640))
AXES = (("z", "x", "y"), ("x", "y", "z"), ("y", "z", "x"))
BLOCK = 128
CAP = 10
UNIT = 8 * CAP
GROUP = 4 * UNIT


def position():
    ep = lax.axis_index("ep")
    return {
        "y": lax.axis_index("batch"),
        "z": lax.axis_index("tp"),
        "x": ep // 2,
        "c": ep % 2,
    }


def moved(me, axis, value):
    there = dict(me)
    there[axis] = value
    return (there["y"], there["z"], there["x"] * 2 + there["c"])


def step(value, distance):
    return lax.rem(value + distance, 4)


def rows_at(index, size):
    return pl.ds(pl.multiple_of(index * size, size), size)


def landed(ref, sem):
    pltpu.make_async_copy(ref, ref, sem).wait()


def push(src, dst, send_sem, recv_sem, device):
    pltpu.make_async_remote_copy(
        src_ref=src,
        dst_ref=dst,
        send_sem=send_sem,
        recv_sem=recv_sem,
        device_id=device,
        device_id_type=MESH,
    ).start()


def routes(me, chunk, weighted, table, select):
    _, axis_b, axis_c = AXES[chunk]

    def body(j, carry):
        there = dict(me)
        there[axis_b] = j // 4
        there[axis_c] = j % 4
        expert = (there["y"] * 4 + there["z"]) * 8 + there["x"] * 2 + there["c"]
        first = expert.astype(jnp.float32) * CAP
        for k in range(8):
            top = (CAP * k) // 8 * 8
            slot = lax.broadcasted_iota(jnp.int32, (16, BLOCK), 0) + (top - CAP * k)
            wanted = jnp.where(
                (slot >= 0) & (slot < CAP), slot.astype(jnp.float32) + first, -1.0
            )
            found = jnp.zeros((16, BLOCK), jnp.float32)
            for q in range(8):
                column = table[chunk, k, q : q + 1, :]
                value = table[chunk, k, 8 + q : 9 + q, :] if weighted else 1.0
                found = jnp.where(wanted == column, value, found)
            parts = [found]
            if top:
                parts.insert(0, jnp.zeros((top, BLOCK), jnp.float32))
            if top < UNIT - 16:
                parts.append(jnp.zeros((UNIT - 16 - top, BLOCK), jnp.float32))
            select[rows_at(j, UNIT), k * BLOCK : (k + 1) * BLOCK] = jnp.concatenate(
                parts, axis=0
            ).astype(jnp.bfloat16)
        return carry

    lax.fori_loop(0, 16, body, 0)


def mixture_kernel(
    rows_ref,
    hidden_ref,
    table_ref,
    swap_ref,
    gate_scale,
    up_scale,
    down_scale,
    gate_hbm,
    up_hbm,
    down_hbm,
    out_ref,
    gate_w,
    up_w,
    down_w,
    table,
    *scratch,
):
    per = 8
    G, O, M, X, N, R, S, H = [scratch[3 * i : 3 * i + 3] for i in range(per)]
    T = scratch[24:27]
    (
        w_sem,
        p_send,
        p_recv,
        pc_send,
        g_send,
        g_recv,
        gc_send,
        b_send,
        b_recv,
        c_send,
        c_recv,
        rc_send,
        rc_recv,
        rb_send,
        rb_recv,
        k_send,
        k_recv,
        t_send,
        t_recv,
    ) = scratch[27:]
    me = position()
    core = me["c"]
    other = (me["y"], me["z"], me["x"] * 2 + (1 - core))

    barrier = pltpu.get_barrier_semaphore()
    for axis in "zxy":
        for d in (1, 2, 3):
            pl.semaphore_signal(
                barrier,
                inc=1,
                device_id=moved(me, axis, step(me[axis], d)),
                device_id_type=MESH,
            )
    pl.semaphore_signal(barrier, inc=1, device_id=other, device_id_type=MESH)
    pl.semaphore_wait(barrier, 10)

    def block_of(a):
        return core * 4 + a

    for chunk, (start, size) in enumerate(CUTS):
        axis = AXES[chunk][0]
        a = me[axis]
        k = block_of(a)
        pltpu.make_async_copy(table_ref, table.at[chunk, k], p_recv.at[chunk, k]).start()
        for d in (1, 3, 2):
            push(
                table_ref,
                table.at[chunk, k],
                p_send.at[chunk, d],
                p_recv.at[chunk, k],
                moved(me, axis, step(a, d)),
            )
    for chunk, (start, size) in enumerate(CUTS):
        axis = AXES[chunk][0]
        a = me[axis]
        k = block_of(a)
        mine = rows_ref.at[:, pl.ds(start, size)]
        place = G[chunk].at[rows_at(k, BLOCK)]
        pltpu.make_async_copy(mine, place, g_recv.at[chunk, k]).start()
        for d in (1, 3, 2):
            push(
                mine,
                place,
                g_send.at[chunk, d],
                g_recv.at[chunk, k],
                moved(me, axis, step(a, d)),
            )
    for n, (src, dst) in enumerate(((gate_hbm, gate_w), (up_hbm, up_w), (down_hbm, down_w))):
        pltpu.make_async_copy(src, dst, w_sem.at[n]).start()
    for d in (0, 1, 3, 2):
        for chunk in range(3):
            k = block_of(step(me[AXES[chunk][0]], d))
            landed(table.at[chunk, k], p_recv.at[chunk, k])
            push(
                table.at[chunk, k],
                table.at[chunk, k],
                pc_send.at[chunk, d],
                p_recv.at[chunk, k],
                other,
            )
    for chunk in range(3):
        for a in range(4):
            k = (1 - core) * 4 + a
            landed(table.at[chunk, k], p_recv.at[chunk, k])
        routes(me, chunk, False, table, S[chunk])
    for d in (0, 1, 3, 2):
        for chunk in range(3):
            k = block_of(step(me[AXES[chunk][0]], d))
            place = G[chunk].at[rows_at(k, BLOCK)]
            landed(place, g_recv.at[chunk, k])
            push(place, place, gc_send.at[chunk, d], g_recv.at[chunk, k], other)

    for chunk in range(3):
        axis = AXES[chunk][1]
        for a in range(4):
            k = (1 - core) * 4 + a
            landed(G[chunk].at[rows_at(k, BLOCK)], g_recv.at[chunk, k])

        def pick(n, carry, chunk=chunk, axis=axis):
            mine = me[axis]
            beta = step(mine, n + 1)
            O[chunk][beta] = jnp.dot(
                S[chunk][rows_at(beta, GROUP), :],
                G[chunk][...],
                preferred_element_type=jnp.float32,
            ).astype(jnp.bfloat16)

            @pl.when(n < 3)
            def _():
                push(
                    O[chunk].at[beta],
                    M[chunk].at[mine],
                    b_send.at[chunk, n],
                    b_recv.at[chunk, mine],
                    moved(me, axis, beta),
                )

            @pl.when(n == 3)
            def _():
                pltpu.make_async_copy(
                    O[chunk].at[beta], M[chunk].at[mine], b_recv.at[chunk, mine]
                ).start()

            return carry

        lax.fori_loop(0, 4, pick, 0)

    def place_of(chunk, beta, gamma):
        return (beta, gamma) if chunk == 1 else (gamma, beta)

    for d in (0, 1, 3, 2):
        for chunk in range(3):
            _, axis_b, axis_c = AXES[chunk]
            beta = step(me[axis_b], d)
            mine = me[axis_c]
            landed(M[chunk].at[beta], b_recv.at[chunk, beta])
            i, j = place_of(chunk, beta, mine)
            for e in (1, 3, 2, 0):
                gamma = step(mine, e)
                src = M[chunk].at[beta, rows_at(gamma, UNIT)]
                dst = X[chunk].at[i, rows_at(j, UNIT)]
                if e:
                    push(
                        src,
                        dst,
                        c_send.at[chunk, d * 4 + e],
                        c_recv.at[chunk, i * 4 + j],
                        moved(me, axis_c, gamma),
                    )
                else:
                    pltpu.make_async_copy(src, dst, c_recv.at[chunk, i * 4 + j]).start()

    for chunk, (start, size) in enumerate(CUTS):
        for d in (1, 2, 3):
            landed(table_ref, p_send.at[chunk, d])
            landed(rows_ref.at[:, pl.ds(start, size)], g_send.at[chunk, d])
        for d in range(4):
            landed(table_ref, pc_send.at[chunk, d])
            landed(G[chunk].at[pl.ds(0, BLOCK)], gc_send.at[chunk, d])
        for n in range(3):
            landed(O[chunk].at[0], b_send.at[chunk, n])
    for n, dst in enumerate((gate_w, up_w, down_w)):
        landed(dst, w_sem.at[n])
    for chunk in (2, 1, 0):
        for i in range(4):
            for j in range(4):
                landed(X[chunk].at[i, pl.ds(j * UNIT, UNIT)], c_recv.at[chunk, i * 4 + j])
        for d in range(4):
            for e in (1, 2, 3):
                landed(X[chunk].at[0, pl.ds(0, UNIT)], c_send.at[chunk, d * 4 + e])

    swap = swap_ref[...]

    def regroup(i, carry):
        turned = jnp.dot(swap, X[2][i], preferred_element_type=jnp.float32).astype(jnp.bfloat16)
        for n in range(4):
            M[2][n, rows_at(i, UNIT), :] = turned[n * UNIT : (n + 1) * UNIT]
        return carry

    lax.fori_loop(0, 4, regroup, 0)

    def expert(n, carry):
        y = step(me["y"], n + 1)
        first = X[0][y]
        second = jnp.dot(swap, X[1][y], preferred_element_type=jnp.float32).astype(jnp.bfloat16)
        third = M[2][y]

        def project(w):
            total = None
            for part, (start, size) in zip((first, second, third), CUTS):
                term = jnp.dot(
                    part, w[start : start + size, :], preferred_element_type=jnp.float32
                )
                total = term if total is None else total + term
            return total

        gate = project(gate_w) * gate_scale[...]
        up = project(up_w) * up_scale[...]
        activated = (gate / (1.0 + jnp.exp(-gate)) * up).astype(jnp.bfloat16)

        def finish(chunk):
            start, size = CUTS[chunk]
            return (
                jnp.dot(
                    activated, down_w[:, start : start + size], preferred_element_type=jnp.float32
                )
                * down_scale[:, start : start + size]
            ).astype(jnp.bfloat16)

        O[0][y] = finish(0)

        @pl.when(n < 3)
        def _():
            push(
                O[0].at[y],
                N[0].at[me["y"]],
                rc_send.at[0, n],
                rc_recv.at[0, me["y"]],
                moved(me, "y", y),
            )

        @pl.when(n == 3)
        def _():
            pltpu.make_async_copy(O[0].at[y], N[0].at[me["y"]], rc_recv.at[0, me["y"]]).start()

        O[1][y] = jnp.dot(swap, finish(1), preferred_element_type=jnp.float32).astype(jnp.bfloat16)
        for e in (1, 3, 2, 0):
            z = step(me["z"], e)
            src = O[1].at[y, rows_at(z, UNIT)]
            dst = N[1].at[me["z"], rows_at(y, UNIT)]
            if e:
                push(
                    src,
                    dst,
                    rc_send.at[1, n * 4 + e],
                    rc_recv.at[1, me["z"] * 4 + y],
                    moved(me, "z", z),
                )
            else:
                pltpu.make_async_copy(src, dst, rc_recv.at[1, me["z"] * 4 + y]).start()
        X[2][y] = finish(2)
        return carry

    lax.fori_loop(0, 4, expert, 0)

    def restore(n, carry):
        mine = me["x"]
        x = step(mine, n + 1)
        parts = jnp.concatenate([X[2][y, rows_at(x, UNIT), :] for y in range(4)], axis=0)
        O[2][x] = jnp.dot(swap, parts, preferred_element_type=jnp.float32).astype(jnp.bfloat16)

        @pl.when(n < 3)
        def _():
            push(
                O[2].at[x],
                N[2].at[mine],
                rc_send.at[2, n],
                rc_recv.at[2, mine],
                moved(me, "x", x),
            )

        @pl.when(n == 3)
        def _():
            pltpu.make_async_copy(O[2].at[x], N[2].at[mine], rc_recv.at[2, mine]).start()

        return carry

    lax.fori_loop(0, 4, restore, 0)

    for chunk in range(3):
        routes(me, chunk, True, table, S[chunk])
    for d in (0, 1, 3, 2):
        for chunk in range(3):
            _, axis_b, axis_c = AXES[chunk]
            gamma = step(me[axis_c], d)
            mine = me[axis_b]
            if chunk == 1:
                for n in range(4):
                    landed(N[1].at[gamma, pl.ds(n * UNIT, UNIT)], rc_recv.at[1, gamma * 4 + n])
            else:
                landed(N[chunk].at[gamma], rc_recv.at[chunk, gamma])
            for e in (1, 3, 2, 0):
                beta = step(mine, e)
                src = N[chunk].at[gamma, rows_at(beta, UNIT)]
                dst = R[chunk].at[rows_at(mine * 4 + gamma, UNIT)]
                if e:
                    push(
                        src,
                        dst,
                        rb_send.at[chunk, d * 4 + e],
                        rb_recv.at[chunk, mine * 4 + gamma],
                        moved(me, axis_b, beta),
                    )
                else:
                    pltpu.make_async_copy(src, dst, rb_recv.at[chunk, mine * 4 + gamma]).start()

    def total(chunk, half):
        return lax.dot_general(
            S[chunk][:, rows_at(half, 512)],
            R[chunk][...],
            (((0,), (0,)), ((), ())),
            preferred_element_type=jnp.float32,
        )

    for chunk in range(3):
        for j in range(16):
            landed(R[chunk].at[pl.ds(j * UNIT, UNIT)], rb_recv.at[chunk, j])
        G[chunk][512:, :] = total(chunk, 1 - core).astype(jnp.bfloat16)
        push(G[chunk].at[pl.ds(512, 512)], H[chunk], k_send.at[chunk], k_recv.at[chunk], other)
    for chunk in range(3):
        axis = AXES[chunk][0]
        mine = me[axis]
        own = total(chunk, core)
        landed(H[chunk], k_recv.at[chunk])
        G[chunk][:512, :] = (own + H[chunk][...].astype(jnp.float32)).astype(jnp.bfloat16)
        for d in (1, 3, 2):
            a = step(mine, d)
            push(
                G[chunk].at[rows_at(a, BLOCK)],
                T[chunk].at[d - 1],
                t_send.at[chunk, d - 1],
                t_recv.at[chunk, d - 1],
                moved(me, axis, a),
            )
    for chunk, (start, size) in enumerate(CUTS):
        mine = me[AXES[chunk][0]]
        result = hidden_ref[:, start : start + size] + G[chunk][rows_at(mine, BLOCK), :].astype(
            jnp.float32
        )
        for d in range(3):
            landed(T[chunk].at[d], t_recv.at[chunk, d])
            result = result + T[chunk][d].astype(jnp.float32)
        out_ref[:, start : start + size] = result.astype(jnp.bfloat16)

    for chunk in range(3):
        for n in range(3):
            if chunk != 1:
                landed(O[chunk].at[0], rc_send.at[chunk, n])
            landed(T[chunk].at[0], t_send.at[chunk, n])
        if chunk == 1:
            for n in range(4):
                for e in (1, 2, 3):
                    landed(O[1].at[0, pl.ds(0, UNIT)], rc_send.at[1, n * 4 + e])
        landed(H[chunk], k_send.at[chunk])
        for d in range(4):
            for e in (1, 2, 3):
                landed(R[chunk].at[pl.ds(0, UNIT)], rb_send.at[chunk, d * 4 + e])


def mixture(rows, hidden, table, gate_s, up_s, down_s, gate_w, up_w, down_w):
    line = np.arange(GROUP)
    a, r = line // UNIT, line % UNIT
    source = ((r % 40) // CAP) * UNIT + (r // 40) * 40 + a * CAP + r % CAP
    swap = jnp.asarray(source[:, None] == line[None, :], jnp.bfloat16)
    dma = pltpu.SemaphoreType.DMA
    width, inner = gate_w.shape

    def each(shape):
        return [pltpu.VMEM(shape + (size,), jnp.bfloat16) for _, size in CUTS]

    vmem = pl.BlockSpec(memory_space=pltpu.VMEM)
    hbm = pl.BlockSpec(memory_space=pl.ANY)
    return pl.pallas_call(
        mixture_kernel,
        out_shape=jax.ShapeDtypeStruct(rows.shape, jnp.bfloat16),
        in_specs=[vmem] * 7 + [hbm] * 3,
        out_specs=vmem,
        scratch_shapes=[
            pltpu.VMEM((width, inner), jnp.bfloat16),
            pltpu.VMEM((width, inner), jnp.bfloat16),
            pltpu.VMEM((inner, width), jnp.bfloat16),
            pltpu.VMEM((3, 8, 16, BLOCK), jnp.float32),
            *each((8 * BLOCK,)),
            *each((4, GROUP)),
            *each((4, GROUP)),
            *each((4, GROUP)),
            *each((4, GROUP)),
            *each((4 * GROUP,)),
            *[pltpu.VMEM((4 * GROUP, 8 * BLOCK), jnp.bfloat16) for _ in CUTS],
            *each((4 * BLOCK,)),
            *each((3, BLOCK)),
            dma((3,)),
            dma((3, 4)),
            dma((3, 8)),
            dma((3, 4)),
            dma((3, 4)),
            dma((3, 8)),
            dma((3, 4)),
            dma((3, 4)),
            dma((3, 4)),
            dma((3, 16)),
            dma((3, 16)),
            dma((3, 16)),
            dma((3, 16)),
            dma((3, 16)),
            dma((3, 16)),
            dma((3,)),
            dma((3,)),
            dma((3, 3)),
            dma((3, 3)),
        ],
        compiler_params=pltpu.CompilerParams(
            collective_id=1, has_side_effects=True, vmem_limit_bytes=64000000
        ),
        cost_estimate=pl.CostEstimate(flops=25 * 10**9, bytes_accessed=12 * 10**6, transcendentals=0),
        name="mixture",
    )(rows, hidden, table, swap, gate_s, up_s, down_s, gate_w, up_w, down_w)


def shards(
    states,
    input_gain,
    query_weight,
    key_weight,
    value_weight,
    query_gain,
    key_gain,
    output_weight,
    mixture_gain,
    expert_gate,
    expert_up,
    expert_down,
    gate_scale,
    up_scale,
    down_scale,
    expert_index,
    expert_slot,
    route_weight,
):
    pair_count, length, features = states.shape
    context = attend(
        states, input_gain, query_weight, key_weight, value_weight, query_gain, key_gain
    )
    head_width = context.shape[2]
    tp_count = lax.axis_size("tp")
    block_rows = length // tp_count
    ordered = jnp.transpose(context, (1, 0, 2)).reshape(length * pair_count, head_width)
    own_rows = lax.psum_scatter(
        jnp.dot(ordered, output_weight, preferred_element_type=jnp.float32).astype(jnp.bfloat16),
        "tp",
        scatter_dimension=0,
        tiled=True,
    ).astype(jnp.float32)
    own_states = lax.dynamic_slice_in_dim(states, lax.axis_index("tp") * block_rows, block_rows, 1)
    hidden_state = own_states.astype(jnp.float32) + jnp.transpose(
        own_rows.reshape(block_rows, pair_count, features), (1, 0, 2)
    )
    expert_input = rms_scale(hidden_state, mixture_gain).astype(jnp.bfloat16)
    columns = (expert_index[0] * CAP + expert_slot[0]).astype(jnp.float32)
    table = jnp.concatenate([columns.T, route_weight[0].T], axis=0)
    result = mixture(
        expert_input[0],
        hidden_state[0],
        table,
        gate_scale,
        up_scale,
        down_scale,
        expert_gate[0],
        expert_up[0],
        expert_down[0],
    )
    return result[None]


def solution(mesh):
    return jax.shard_map(
        shards,
        mesh=mesh,
        in_specs=(
            P(("batch", "ep"), None, None),
            P(),
            P(None, "tp"),
            P(None, "tp"),
            P(None, "tp"),
            P(),
            P(),
            P("tp", None),
            P(),
            P(("batch", "tp", "ep"), None, None),
            P(("batch", "tp", "ep"), None, None),
            P(("batch", "tp", "ep"), None, None),
            P(("batch", "tp", "ep"), None),
            P(("batch", "tp", "ep"), None),
            P(("batch", "tp", "ep"), None),
            P(("batch", "ep"), "tp", None),
            P(("batch", "ep"), "tp", None),
            P(("batch", "ep"), "tp", None),
        ),
        out_specs=P(("batch", "ep"), "tp", None),
        check_vma=False,
    )
```

```python
import math

import jax
import jax.numpy as jnp
import numpy as np
from jax import lax
from jax.experimental import pallas as pl
from jax.experimental.pallas import tpu as pltpu
from jax.sharding import PartitionSpec as P

MESH = pl.DeviceIdType.MESH
CUTS = ((0, 768), (768, 640), (1408, 640))
AXES = (("z", "x", "y"), ("x", "y", "z"), ("y", "z", "x"))
BLOCK = 128
CAP = 10
UNIT = 8 * CAP
GROUP = 4 * UNIT


def position():
    ep = lax.axis_index("ep")
    return {
        "y": lax.axis_index("batch"),
        "z": lax.axis_index("tp"),
        "x": ep // 2,
        "c": ep % 2,
    }


def moved(me, axis, value):
    there = dict(me)
    there[axis] = value
    return (there["y"], there["z"], there["x"] * 2 + there["c"])


def step(value, distance):
    return lax.rem(value + distance, 4)


def rows_at(index, size):
    return pl.ds(pl.multiple_of(index * size, size), size)


def landed(ref, sem):
    pltpu.make_async_copy(ref, ref, sem).wait()


def push(src, dst, send_sem, recv_sem, device):
    pltpu.make_async_remote_copy(
        src_ref=src,
        dst_ref=dst,
        send_sem=send_sem,
        recv_sem=recv_sem,
        device_id=device,
        device_id_type=MESH,
    ).start()


def routes(me, chunk, weighted, table, select):
    _, axis_b, axis_c = AXES[chunk]

    def body(j, carry):
        there = dict(me)
        there[axis_b] = j // 4
        there[axis_c] = j % 4
        expert = (there["y"] * 4 + there["z"]) * 8 + there["x"] * 2 + there["c"]
        first = expert.astype(jnp.float32) * CAP
        for k in range(8):
            top = (CAP * k) // 8 * 8
            slot = lax.broadcasted_iota(jnp.int32, (16, BLOCK), 0) + (top - CAP * k)
            wanted = jnp.where(
                (slot >= 0) & (slot < CAP), slot.astype(jnp.float32) + first, -1.0
            )
            found = jnp.zeros((16, BLOCK), jnp.float32)
            for q in range(8):
                column = table[chunk, k, q : q + 1, :]
                value = table[chunk, k, 8 + q : 9 + q, :] if weighted else 1.0
                found = jnp.where(wanted == column, value, found)
            parts = [found]
            if top:
                parts.insert(0, jnp.zeros((top, BLOCK), jnp.float32))
            if top < UNIT - 16:
                parts.append(jnp.zeros((UNIT - 16 - top, BLOCK), jnp.float32))
            select[rows_at(j, UNIT), k * BLOCK : (k + 1) * BLOCK] = jnp.concatenate(
                parts, axis=0
            ).astype(jnp.bfloat16)
        return carry

    lax.fori_loop(0, 16, body, 0)


def mixture_kernel(
    rows_ref,
    hidden_ref,
    table_ref,
    swap_ref,
    gate_scale,
    up_scale,
    down_scale,
    gate_hbm,
    up_hbm,
    down_hbm,
    out_ref,
    gate_w,
    up_w,
    down_w,
    table,
    *scratch,
):
    per = 8
    G, O, M, X, N, R, S, H = [scratch[3 * i : 3 * i + 3] for i in range(per)]
    T = scratch[24:27]
    (
        w_sem,
        p_send,
        p_recv,
        pc_send,
        g_send,
        g_recv,
        gc_send,
        b_send,
        b_recv,
        c_send,
        c_recv,
        rc_send,
        rc_recv,
        rb_send,
        rb_recv,
        k_send,
        k_recv,
        t_send,
        t_recv,
    ) = scratch[27:]
    me = position()
    core = me["c"]
    other = (me["y"], me["z"], me["x"] * 2 + (1 - core))

    barrier = pltpu.get_barrier_semaphore()
    for axis in "zxy":
        for d in (1, 2, 3):
            pl.semaphore_signal(
                barrier,
                inc=1,
                device_id=moved(me, axis, step(me[axis], d)),
                device_id_type=MESH,
            )
    pl.semaphore_signal(barrier, inc=1, device_id=other, device_id_type=MESH)
    pl.semaphore_wait(barrier, 10)

    def block_of(a):
        return core * 4 + a

    for chunk, (start, size) in enumerate(CUTS):
        axis = AXES[chunk][0]
        a = me[axis]
        k = block_of(a)
        pltpu.make_async_copy(table_ref, table.at[chunk, k], p_recv.at[chunk, k]).start()
        for d in (1, 3, 2):
            push(
                table_ref,
                table.at[chunk, k],
                p_send.at[chunk, d],
                p_recv.at[chunk, k],
                moved(me, axis, step(a, d)),
            )
    for chunk, (start, size) in enumerate(CUTS):
        axis = AXES[chunk][0]
        a = me[axis]
        k = block_of(a)
        mine = rows_ref.at[:, pl.ds(start, size)]
        place = G[chunk].at[rows_at(k, BLOCK)]
        pltpu.make_async_copy(mine, place, g_recv.at[chunk, k]).start()
        for d in (1, 3, 2):
            push(
                mine,
                place,
                g_send.at[chunk, d],
                g_recv.at[chunk, k],
                moved(me, axis, step(a, d)),
            )
    for n, (src, dst) in enumerate(((gate_hbm, gate_w), (up_hbm, up_w), (down_hbm, down_w))):
        pltpu.make_async_copy(src, dst, w_sem.at[n]).start()
    for d in (0, 1, 3, 2):
        for chunk in range(3):
            k = block_of(step(me[AXES[chunk][0]], d))
            landed(table.at[chunk, k], p_recv.at[chunk, k])
            push(
                table.at[chunk, k],
                table.at[chunk, k],
                pc_send.at[chunk, d],
                p_recv.at[chunk, k],
                other,
            )
    for chunk in range(3):
        for a in range(4):
            k = (1 - core) * 4 + a
            landed(table.at[chunk, k], p_recv.at[chunk, k])
        routes(me, chunk, False, table, S[chunk])
    for d in (0, 1, 3, 2):
        for chunk in range(3):
            k = block_of(step(me[AXES[chunk][0]], d))
            place = G[chunk].at[rows_at(k, BLOCK)]
            landed(place, g_recv.at[chunk, k])
            push(place, place, gc_send.at[chunk, d], g_recv.at[chunk, k], other)

    for chunk in range(3):
        axis = AXES[chunk][1]
        for a in range(4):
            k = (1 - core) * 4 + a
            landed(G[chunk].at[rows_at(k, BLOCK)], g_recv.at[chunk, k])

        def pick(n, carry, chunk=chunk, axis=axis):
            mine = me[axis]
            beta = step(mine, n + 1)
            O[chunk][beta] = jnp.dot(
                S[chunk][rows_at(beta, GROUP), :],
                G[chunk][...],
                preferred_element_type=jnp.float32,
            ).astype(jnp.bfloat16)

            @pl.when(n < 3)
            def _():
                push(
                    O[chunk].at[beta],
                    M[chunk].at[mine],
                    b_send.at[chunk, n],
                    b_recv.at[chunk, mine],
                    moved(me, axis, beta),
                )

            @pl.when(n == 3)
            def _():
                pltpu.make_async_copy(
                    O[chunk].at[beta], M[chunk].at[mine], b_recv.at[chunk, mine]
                ).start()

            return carry

        lax.fori_loop(0, 4, pick, 0)

    def place_of(chunk, beta, gamma):
        return (beta, gamma) if chunk == 1 else (gamma, beta)

    for d in (0, 1, 3, 2):
        for chunk in range(3):
            _, axis_b, axis_c = AXES[chunk]
            beta = step(me[axis_b], d)
            mine = me[axis_c]
            landed(M[chunk].at[beta], b_recv.at[chunk, beta])
            i, j = place_of(chunk, beta, mine)
            for e in (1, 3, 2, 0):
                gamma = step(mine, e)
                src = M[chunk].at[beta, rows_at(gamma, UNIT)]
                dst = X[chunk].at[i, rows_at(j, UNIT)]
                if e:
                    push(
                        src,
                        dst,
                        c_send.at[chunk, d * 4 + e],
                        c_recv.at[chunk, i * 4 + j],
                        moved(me, axis_c, gamma),
                    )
                else:
                    pltpu.make_async_copy(src, dst, c_recv.at[chunk, i * 4 + j]).start()

    for chunk, (start, size) in enumerate(CUTS):
        for d in (1, 2, 3):
            landed(table_ref, p_send.at[chunk, d])
            landed(rows_ref.at[:, pl.ds(start, size)], g_send.at[chunk, d])
        for d in range(4):
            landed(table_ref, pc_send.at[chunk, d])
            landed(G[chunk].at[pl.ds(0, BLOCK)], gc_send.at[chunk, d])
        for n in range(3):
            landed(O[chunk].at[0], b_send.at[chunk, n])
    for n, dst in enumerate((gate_w, up_w, down_w)):
        landed(dst, w_sem.at[n])
    for chunk in (2, 1, 0):
        for i in range(4):
            for j in range(4):
                landed(X[chunk].at[i, pl.ds(j * UNIT, UNIT)], c_recv.at[chunk, i * 4 + j])
        for d in range(4):
            for e in (1, 2, 3):
                landed(X[chunk].at[0, pl.ds(0, UNIT)], c_send.at[chunk, d * 4 + e])

    swap = swap_ref[...]

    def regroup(i, carry):
        turned = jnp.dot(swap, X[2][i], preferred_element_type=jnp.float32).astype(jnp.bfloat16)
        for n in range(4):
            M[2][n, rows_at(i, UNIT), :] = turned[n * UNIT : (n + 1) * UNIT]
        return carry

    lax.fori_loop(0, 4, regroup, 0)

    def expert(n, carry):
        y = step(me["y"], n + 1)
        first = X[0][y]
        second = jnp.dot(swap, X[1][y], preferred_element_type=jnp.float32).astype(jnp.bfloat16)
        third = M[2][y]

        def project(w):
            total = None
            for part, (start, size) in zip((first, second, third), CUTS):
                term = jnp.dot(
                    part, w[start : start + size, :], preferred_element_type=jnp.float32
                )
                total = term if total is None else total + term
            return total

        gate = project(gate_w) * gate_scale[...]
        up = project(up_w) * up_scale[...]
        activated = (gate / (1.0 + jnp.exp(-gate)) * up).astype(jnp.bfloat16)

        def finish(chunk):
            start, size = CUTS[chunk]
            return (
                jnp.dot(
                    activated, down_w[:, start : start + size], preferred_element_type=jnp.float32
                )
                * down_scale[:, start : start + size]
            ).astype(jnp.bfloat16)

        O[0][y] = finish(0)

        @pl.when(n < 3)
        def _():
            push(
                O[0].at[y],
                N[0].at[me["y"]],
                rc_send.at[0, n],
                rc_recv.at[0, me["y"]],
                moved(me, "y", y),
            )

        @pl.when(n == 3)
        def _():
            pltpu.make_async_copy(O[0].at[y], N[0].at[me["y"]], rc_recv.at[0, me["y"]]).start()

        O[1][y] = jnp.dot(swap, finish(1), preferred_element_type=jnp.float32).astype(jnp.bfloat16)
        for e in (1, 3, 2, 0):
            z = step(me["z"], e)
            src = O[1].at[y, rows_at(z, UNIT)]
            dst = N[1].at[me["z"], rows_at(y, UNIT)]
            if e:
                push(
                    src,
                    dst,
                    rc_send.at[1, n * 4 + e],
                    rc_recv.at[1, me["z"] * 4 + y],
                    moved(me, "z", z),
                )
            else:
                pltpu.make_async_copy(src, dst, rc_recv.at[1, me["z"] * 4 + y]).start()
        X[2][y] = finish(2)
        return carry

    lax.fori_loop(0, 4, expert, 0)

    def restore(n, carry):
        mine = me["x"]
        x = step(mine, n + 1)
        parts = jnp.concatenate([X[2][y, rows_at(x, UNIT), :] for y in range(4)], axis=0)
        O[2][x] = jnp.dot(swap, parts, preferred_element_type=jnp.float32).astype(jnp.bfloat16)

        @pl.when(n < 3)
        def _():
            push(
                O[2].at[x],
                N[2].at[mine],
                rc_send.at[2, n],
                rc_recv.at[2, mine],
                moved(me, "x", x),
            )

        @pl.when(n == 3)
        def _():
            pltpu.make_async_copy(O[2].at[x], N[2].at[mine], rc_recv.at[2, mine]).start()

        return carry

    lax.fori_loop(0, 4, restore, 0)

    for chunk in range(3):
        routes(me, chunk, True, table, S[chunk])
    for d in (0, 1, 3, 2):
        for chunk in range(3):
            _, axis_b, axis_c = AXES[chunk]
            gamma = step(me[axis_c], d)
            mine = me[axis_b]
            if chunk == 1:
                for n in range(4):
                    landed(N[1].at[gamma, pl.ds(n * UNIT, UNIT)], rc_recv.at[1, gamma * 4 + n])
            else:
                landed(N[chunk].at[gamma], rc_recv.at[chunk, gamma])
            for e in (1, 3, 2, 0):
                beta = step(mine, e)
                src = N[chunk].at[gamma, rows_at(beta, UNIT)]
                dst = R[chunk].at[rows_at(mine * 4 + gamma, UNIT)]
                if e:
                    push(
                        src,
                        dst,
                        rb_send.at[chunk, d * 4 + e],
                        rb_recv.at[chunk, mine * 4 + gamma],
                        moved(me, axis_b, beta),
                    )
                else:
                    pltpu.make_async_copy(src, dst, rb_recv.at[chunk, mine * 4 + gamma]).start()

    def total(chunk, half):
        return lax.dot_general(
            S[chunk][:, rows_at(half, 512)],
            R[chunk][...],
            (((0,), (0,)), ((), ())),
            preferred_element_type=jnp.float32,
        )

    for chunk in range(3):
        for j in range(16):
            landed(R[chunk].at[pl.ds(j * UNIT, UNIT)], rb_recv.at[chunk, j])
        G[chunk][512:, :] = total(chunk, 1 - core).astype(jnp.bfloat16)
        push(G[chunk].at[pl.ds(512, 512)], H[chunk], k_send.at[chunk], k_recv.at[chunk], other)
    for chunk in range(3):
        axis = AXES[chunk][0]
        mine = me[axis]
        own = total(chunk, core)
        landed(H[chunk], k_recv.at[chunk])
        G[chunk][:512, :] = (own + H[chunk][...].astype(jnp.float32)).astype(jnp.bfloat16)
        for d in (1, 3, 2):
            a = step(mine, d)
            push(
                G[chunk].at[rows_at(a, BLOCK)],
                T[chunk].at[d - 1],
                t_send.at[chunk, d - 1],
                t_recv.at[chunk, d - 1],
                moved(me, axis, a),
            )
    for chunk, (start, size) in enumerate(CUTS):
        mine = me[AXES[chunk][0]]
        result = hidden_ref[:, start : start + size] + G[chunk][rows_at(mine, BLOCK), :].astype(
            jnp.float32
        )
        for d in range(3):
            landed(T[chunk].at[d], t_recv.at[chunk, d])
            result = result + T[chunk][d].astype(jnp.float32)
        out_ref[:, start : start + size] = result.astype(jnp.bfloat16)

    for chunk in range(3):
        for n in range(3):
            if chunk != 1:
                landed(O[chunk].at[0], rc_send.at[chunk, n])
            landed(T[chunk].at[0], t_send.at[chunk, n])
        if chunk == 1:
            for n in range(4):
                for e in (1, 2, 3):
                    landed(O[1].at[0, pl.ds(0, UNIT)], rc_send.at[1, n * 4 + e])
        landed(H[chunk], k_send.at[chunk])
        for d in range(4):
            for e in (1, 2, 3):
                landed(R[chunk].at[pl.ds(0, UNIT)], rb_send.at[chunk, d * 4 + e])


def mixture(rows, hidden, table, gate_s, up_s, down_s, gate_w, up_w, down_w):
    line = np.arange(GROUP)
    a, r = line // UNIT, line % UNIT
    source = ((r % 40) // CAP) * UNIT + (r // 40) * 40 + a * CAP + r % CAP
    swap = jnp.asarray(source[:, None] == line[None, :], jnp.bfloat16)
    dma = pltpu.SemaphoreType.DMA
    width, inner = gate_w.shape

    def each(shape):
        return [pltpu.VMEM(shape + (size,), jnp.bfloat16) for _, size in CUTS]

    vmem = pl.BlockSpec(memory_space=pltpu.VMEM)
    hbm = pl.BlockSpec(memory_space=pl.ANY)
    return pl.pallas_call(
        mixture_kernel,
        out_shape=jax.ShapeDtypeStruct(rows.shape, jnp.bfloat16),
        in_specs=[vmem] * 7 + [hbm] * 3,
        out_specs=vmem,
        scratch_shapes=[
            pltpu.VMEM((width, inner), jnp.bfloat16),
            pltpu.VMEM((width, inner), jnp.bfloat16),
            pltpu.VMEM((inner, width), jnp.bfloat16),
            pltpu.VMEM((3, 8, 16, BLOCK), jnp.float32),
            *each((8 * BLOCK,)),
            *each((4, GROUP)),
            *each((4, GROUP)),
            *each((4, GROUP)),
            *each((4, GROUP)),
            *each((4 * GROUP,)),
            *[pltpu.VMEM((4 * GROUP, 8 * BLOCK), jnp.bfloat16) for _ in CUTS],
            *each((4 * BLOCK,)),
            *each((3, BLOCK)),
            dma((3,)),
            dma((3, 4)),
            dma((3, 8)),
            dma((3, 4)),
            dma((3, 4)),
            dma((3, 8)),
            dma((3, 4)),
            dma((3, 4)),
            dma((3, 4)),
            dma((3, 16)),
            dma((3, 16)),
            dma((3, 16)),
            dma((3, 16)),
            dma((3, 16)),
            dma((3, 16)),
            dma((3,)),
            dma((3,)),
            dma((3, 3)),
            dma((3, 3)),
        ],
        compiler_params=pltpu.CompilerParams(
            collective_id=1, has_side_effects=True, vmem_limit_bytes=64000000
        ),
        cost_estimate=pl.CostEstimate(flops=25 * 10**9, bytes_accessed=12 * 10**6, transcendentals=0),
        name="mixture",
    )(rows, hidden, table, swap, gate_s, up_s, down_s, gate_w, up_w, down_w)


EPS = 1e-06
SEQ = 512
HEAD = 128


def attention_kernel(
    states_hbm,
    input_gain,
    query_gain,
    key_gain,
    cosine,
    sine,
    mixture_gain,
    query_hbm,
    key_hbm,
    value_hbm,
    output_hbm,
    rows_out,
    hidden_out,
    states,
    normed,
    query_w,
    kv_w,
    output_w,
    queries,
    keys,
    values,
    context,
    leaving,
    halves,
    arrived,
    load_sem,
    half_send,
    half_recv,
    full_send,
    full_recv,
):
    me = position()
    z = me["z"]
    width = states.shape[1]
    half = width // 2
    heads = query_w.shape[1] // HEAD
    ahead = moved(me, "z", step(z, 1))
    behind = moved(me, "z", step(z, 3))
    barrier = pltpu.get_barrier_semaphore()
    for neighbour in (ahead, behind):
        pl.semaphore_signal(barrier, inc=1, device_id=neighbour, device_id_type=MESH)

    loads = [
        pltpu.make_async_copy(src, dst, load_sem.at[n])
        for n, (src, dst) in enumerate(
            (
                (states_hbm, states),
                (key_hbm, kv_w.at[:, pl.ds(0, HEAD)]),
                (value_hbm, kv_w.at[:, pl.ds(HEAD, HEAD)]),
                (query_hbm, query_w),
                (output_hbm, output_w),
            )
        )
    ]
    for load in loads:
        load.start()

    loads[0].wait()

    def norm(i, carry):
        part = states[rows_at(i, 128), :].astype(jnp.float32)
        scale = lax.rsqrt(jnp.mean(part * part, axis=-1, keepdims=True) + EPS)
        normed[rows_at(i, 128), :] = (part * scale * input_gain[...]).astype(jnp.bfloat16)
        return carry

    lax.fori_loop(0, SEQ // 128, norm, 0)

    def turn(part, gain, factor):
        scale = lax.rsqrt(jnp.mean(part * part, axis=-1, keepdims=True) + EPS) * factor
        part = part * gain
        return (
            (part * cosine[...] + pltpu.roll(part, HEAD // 2, 1) * sine[...]) * scale
        ).astype(jnp.bfloat16)

    loads[1].wait()
    loads[2].wait()
    both = jnp.dot(normed[...], kv_w[...], preferred_element_type=jnp.float32)
    keys[...] = turn(both[:, :HEAD], key_gain[...], 1.0)
    values[:, :HEAD] = both[:, HEAD:].astype(jnp.bfloat16)
    values[:, HEAD:] = jnp.ones((SEQ, HEAD), jnp.bfloat16)
    loads[3].wait()
    factor = math.log2(math.e) / math.sqrt(HEAD)

    def project(n, carry):
        pair = jnp.dot(
            normed[...], query_w[:, rows_at(n, 2 * HEAD)], preferred_element_type=jnp.float32
        )
        for h in range(2):
            head = turn(pair[:, h * HEAD : (h + 1) * HEAD], query_gain[...], factor)
            for i in range(4):
                queries[i, rows_at(2 * n + h, BLOCK), :] = head[i * BLOCK : (i + 1) * BLOCK]
        return carry

    lax.fori_loop(0, heads // 2, project, 0)
    loads[4].wait()
    pl.semaphore_wait(barrier, 2)

    def block(index):
        for n in range(heads // 2):
            scores = lax.dot_general(
                queries[index, n * 2 * BLOCK : (n + 1) * 2 * BLOCK, :],
                keys[...],
                (((1,), (1,)), ((), ())),
                preferred_element_type=jnp.float32,
            )
            mixed = jnp.dot(
                jnp.exp2(scores).astype(jnp.bfloat16),
                values[...],
                preferred_element_type=jnp.float32,
            )
            mixed = (mixed[:, :HEAD] / mixed[:, HEAD:]).astype(jnp.bfloat16)
            for h in range(2):
                context[:, (2 * n + h) * HEAD : (2 * n + h + 1) * HEAD] = mixed[
                    h * BLOCK : (h + 1) * BLOCK
                ]

    def part(side):
        return jnp.dot(
            context[...],
            output_w[:, side * half : (side + 1) * half],
            preferred_element_type=jnp.float32,
        )

    block(step(z, 2))
    for side, device in ((0, ahead), (1, behind)):
        leaving[2, side] = part(side).astype(jnp.bfloat16)
        push(
            leaving.at[2, side], halves.at[side], half_send.at[side], half_recv.at[side], device
        )
    for way, (distance, device) in enumerate(((1, ahead), (3, behind))):
        block(step(z, distance))
        for side in (1 - way, way):
            total = part(side)
            if side == way:
                landed(halves.at[side], half_recv.at[side])
                total = total + halves[side].astype(jnp.float32)
            leaving[way, side] = total.astype(jnp.bfloat16)
            push(
                leaving.at[way, side],
                arrived.at[way, side],
                full_send.at[way, side],
                full_recv.at[way, side],
                device,
            )
    block(z)
    for side in range(2):
        columns = slice(side * half, (side + 1) * half)
        hidden_out[:, columns] = part(side) + states[rows_at(z, BLOCK), columns].astype(
            jnp.float32
        )
    for side in range(2):
        columns = slice(side * half, (side + 1) * half)
        for way in range(2):
            landed(arrived.at[way, side], full_recv.at[way, side])
        hidden_out[:, columns] = hidden_out[:, columns] + (
            arrived[0, side].astype(jnp.float32) + arrived[1, side].astype(jnp.float32)
        )
    hidden = hidden_out[...]
    scale = lax.rsqrt(jnp.mean(hidden * hidden, axis=-1, keepdims=True) + EPS)
    rows_out[...] = (hidden * scale * mixture_gain[...]).astype(jnp.bfloat16)
    for side in range(2):
        landed(halves.at[side], half_send.at[side])
        for way in range(2):
            landed(arrived.at[way, side], full_send.at[way, side])


def attention(
    states, input_gain, query_w, key_w, value_w, query_gain, key_gain, output_w, mixture_gain
):
    length, width = states.shape
    span = query_w.shape[1]
    index = np.arange(HEAD // 2, dtype=np.float64)
    angles = np.arange(length, dtype=np.float64)[:, None] * 1e6 ** (-2.0 * index / HEAD)[None, :]
    cosine = np.concatenate([np.cos(angles)] * 2, axis=1).astype(np.float32)
    sine = np.concatenate([-np.sin(angles), np.sin(angles)], axis=1).astype(np.float32)
    vmem = pl.BlockSpec(memory_space=pltpu.VMEM)
    hbm = pl.BlockSpec(memory_space=pl.ANY)
    dma = pltpu.SemaphoreType.DMA
    half = width // 2
    bf16 = jnp.bfloat16
    return pl.pallas_call(
        attention_kernel,
        out_shape=(
            jax.ShapeDtypeStruct((BLOCK, width), bf16),
            jax.ShapeDtypeStruct((BLOCK, width), jnp.float32),
        ),
        in_specs=[hbm] + [vmem] * 6 + [hbm] * 4,
        out_specs=(vmem, vmem),
        scratch_shapes=[
            pltpu.VMEM((length, width), bf16),
            pltpu.VMEM((length, width), bf16),
            pltpu.VMEM((width, span), bf16),
            pltpu.VMEM((width, 2 * HEAD), bf16),
            pltpu.VMEM((span, width), bf16),
            pltpu.VMEM((4, span, HEAD), bf16),
            pltpu.VMEM((length, HEAD), bf16),
            pltpu.VMEM((length, 2 * HEAD), bf16),
            pltpu.VMEM((BLOCK, span), bf16),
            pltpu.VMEM((3, 2, BLOCK, half), bf16),
            pltpu.VMEM((2, BLOCK, half), bf16),
            pltpu.VMEM((2, 2, BLOCK, half), bf16),
            dma((5,)),
            dma((2,)),
            dma((2,)),
            dma((2, 2)),
            dma((2, 2)),
        ],
        compiler_params=pltpu.CompilerParams(
            collective_id=2, has_side_effects=True, vmem_limit_bytes=48000000
        ),
        cost_estimate=pl.CostEstimate(
            flops=6 * 10**9, bytes_accessed=13 * 10**6, transcendentals=2 * 10**6
        ),
        name="attention",
    )(
        states,
        input_gain[None],
        query_gain[None],
        key_gain[None],
        jnp.asarray(cosine),
        jnp.asarray(sine),
        mixture_gain[None],
        query_w,
        key_w,
        value_w,
        output_w,
    )


def shards(
    states,
    input_gain,
    query_weight,
    key_weight,
    value_weight,
    query_gain,
    key_gain,
    output_weight,
    mixture_gain,
    expert_gate,
    expert_up,
    expert_down,
    gate_scale,
    up_scale,
    down_scale,
    expert_index,
    expert_slot,
    route_weight,
):
    rows, hidden = attention(
        states[0],
        input_gain,
        query_weight,
        key_weight,
        value_weight,
        query_gain,
        key_gain,
        output_weight,
        mixture_gain,
    )
    columns = (expert_index[0] * CAP + expert_slot[0]).astype(jnp.float32)
    table = jnp.concatenate([columns.T, route_weight[0].T], axis=0)
    result = mixture(
        rows,
        hidden,
        table,
        gate_scale,
        up_scale,
        down_scale,
        expert_gate[0],
        expert_up[0],
        expert_down[0],
    )
    return result[None]


def solution(mesh):
    return jax.shard_map(
        shards,
        mesh=mesh,
        in_specs=(
            P(("batch", "ep"), None, None),
            P(),
            P(None, "tp"),
            P(None, "tp"),
            P(None, "tp"),
            P(),
            P(),
            P("tp", None),
            P(),
            P(("batch", "tp", "ep"), None, None),
            P(("batch", "tp", "ep"), None, None),
            P(("batch", "tp", "ep"), None, None),
            P(("batch", "tp", "ep"), None),
            P(("batch", "tp", "ep"), None),
            P(("batch", "tp", "ep"), None),
            P(("batch", "ep"), "tp", None),
            P(("batch", "ep"), "tp", None),
            P(("batch", "ep"), "tp", None),
        ),
        out_specs=P(("batch", "ep"), "tp", None),
        check_vma=False,
    )
```

```python
import math

import jax
import jax.numpy as jnp
import numpy as np
from jax import lax
from jax.experimental import pallas as pl
from jax.experimental.pallas import tpu as pltpu
from jax.sharding import PartitionSpec as P

MESH = pl.DeviceIdType.MESH
SETS = (
    ((0, 512), (768, 384), (1408, 384)),
    ((512, 256), (1152, 256), (1792, 256)),
)
CUTS = tuple(cut for cuts in SETS for cut in cuts)
AXES = (("z", "x", "y"), ("x", "y", "z"), ("y", "z", "x"))
FORTH = tuple(range(len(SETS)))
BACK = FORTH[::-1]
BLOCK = 128
CAP = 10
UNIT = 8 * CAP
GROUP = 4 * UNIT
EPS = 1e-06
SEQ = 512
HEAD = 128


def position():
    ep = lax.axis_index("ep")
    return {
        "y": lax.axis_index("batch"),
        "z": lax.axis_index("tp"),
        "x": ep // 2,
        "c": ep % 2,
    }


def moved(me, axis, value):
    there = dict(me)
    there[axis] = value
    return (there["y"], there["z"], there["x"] * 2 + there["c"])


def step(value, distance):
    return lax.rem(value + distance, 4)


def rows_at(index, size):
    return pl.ds(pl.multiple_of(index * size, size), size)


def landed(ref, sem):
    pltpu.make_async_copy(ref, ref, sem).wait()


def push(src, dst, send_sem, recv_sem, device):
    pltpu.make_async_remote_copy(
        src_ref=src,
        dst_ref=dst,
        send_sem=send_sem,
        recv_sem=recv_sem,
        device_id=device,
        device_id_type=MESH,
    ).start()


def routes(me, group, weighted, table, select):
    _, axis_b, axis_c = AXES[group]

    def body(j, carry):
        there = dict(me)
        there[axis_b] = j // 4
        there[axis_c] = j % 4
        expert = (there["y"] * 4 + there["z"]) * 8 + there["x"] * 2 + there["c"]
        first = expert.astype(jnp.float32) * CAP
        for k in range(8):
            top = (CAP * k) // 8 * 8
            slot = lax.broadcasted_iota(jnp.int32, (16, BLOCK), 0) + (top - CAP * k)
            wanted = jnp.where(
                (slot >= 0) & (slot < CAP), slot.astype(jnp.float32) + first, -1.0
            )
            found = jnp.zeros((16, BLOCK), jnp.float32)
            for q in range(8):
                column = table[group, k, q : q + 1, :]
                value = table[group, k, 8 + q : 9 + q, :] if weighted else 1.0
                found = jnp.where(wanted == column, value, found)
            parts = [found]
            if top:
                parts.insert(0, jnp.zeros((top, BLOCK), jnp.float32))
            if top < UNIT - 16:
                parts.append(jnp.zeros((UNIT - 16 - top, BLOCK), jnp.float32))
            select[rows_at(j, UNIT), k * BLOCK : (k + 1) * BLOCK] = jnp.concatenate(
                parts, axis=0
            ).astype(jnp.bfloat16)
        return carry

    lax.fori_loop(0, 16, body, 0)


def layer_kernel(*refs):
    (
        states_hbm,
        input_gain_hbm,
        query_gain_hbm,
        key_gain_hbm,
        cosine_hbm,
        sine_hbm,
        mixture_gain_hbm,
        query_hbm,
        key_hbm,
        value_hbm,
        output_hbm,
        table_hbm,
        swap_hbm,
        gate_scale_hbm,
        up_scale_hbm,
        down_scale_hbm,
        gate_hbm,
        up_hbm,
        down_hbm,
        out_ref,
        rows_ref,
        hidden_ref,
        table_ref,
        table,
        swap_ref,
        gate_scale,
        up_scale,
        down_scale,
        mixture_gain,
        halves,
        arrived,
    ) = refs[:31]
    count = len(CUTS)
    G, M, X, N, R, H, T = [refs[31 + count * i : 31 + count * (i + 1)] for i in range(7)]
    (
        load_sem,
        small_sem,
        w_sem,
        half_send,
        half_recv,
        full_send,
        full_recv,
        p_send,
        p_recv,
        pc_send,
        g_send,
        g_recv,
        gc_send,
        b_send,
        b_recv,
        c_send,
        c_recv,
        rc_send,
        rc_recv,
        rb_send,
        rb_recv,
        k_send,
        k_recv,
        t_send,
        t_recv,
    ) = refs[31 + 7 * count :]
    me = position()
    z = me["z"]
    core = me["c"]
    other = (me["y"], me["z"], me["x"] * 2 + (1 - core))
    ahead = moved(me, "z", step(z, 1))
    behind = moved(me, "z", step(z, 3))

    barrier = pltpu.get_barrier_semaphore()
    for axis in "zxy":
        for d in (1, 2, 3):
            pl.semaphore_signal(
                barrier,
                inc=1,
                device_id=moved(me, axis, step(me[axis], d)),
                device_id_type=MESH,
            )
    pl.semaphore_signal(barrier, inc=1, device_id=other, device_id_type=MESH)

    def block_of(a):
        return core * 4 + a

    def attention(
        input_gain,
        query_gain,
        key_gain,
        cosine,
        sine,
        states,
        normed,
        query_w,
        kv_w,
        output_w,
        queries,
        keys,
        values,
        context,
        leaving,
    ):
        width = states.shape[1]
        half = width // 2
        heads = query_w.shape[1] // HEAD
        loads = [
            pltpu.make_async_copy(src, dst, load_sem.at[n])
            for n, (src, dst) in enumerate(
                (
                    (states_hbm, states),
                    (input_gain_hbm, input_gain),
                    (key_hbm, kv_w.at[:, pl.ds(0, HEAD)]),
                    (value_hbm, kv_w.at[:, pl.ds(HEAD, HEAD)]),
                    (key_gain_hbm, key_gain),
                    (cosine_hbm, cosine),
                    (sine_hbm, sine),
                    (query_gain_hbm, query_gain),
                    (query_hbm, query_w),
                    (output_hbm, output_w),
                )
            )
        ]
        small = [
            pltpu.make_async_copy(src, dst, small_sem.at[n])
            for n, (src, dst) in enumerate(
                (
                    (table_hbm, table_ref),
                    (mixture_gain_hbm, mixture_gain),
                    (swap_hbm, swap_ref),
                    (gate_scale_hbm, gate_scale),
                    (up_scale_hbm, up_scale),
                    (down_scale_hbm, down_scale),
                )
            )
        ]
        for load in loads + small:
            load.start()
        loads[0].wait()
        loads[1].wait()

        def norm(i, carry):
            part = states[rows_at(i, 128), :].astype(jnp.float32)
            scale = lax.rsqrt(jnp.mean(part * part, axis=-1, keepdims=True) + EPS)
            normed[rows_at(i, 128), :] = (part * scale * input_gain[...]).astype(jnp.bfloat16)
            return carry

        lax.fori_loop(0, SEQ // 128, norm, 0)
        for load in loads[2:7]:
            load.wait()
        def turn(part, gain, factor):
            scale = lax.rsqrt(jnp.mean(part * part, axis=-1, keepdims=True) + EPS) * factor
            part = part * gain
            return (
                (part * cosine[...] + pltpu.roll(part, HEAD // 2, 1) * sine[...]) * scale
            ).astype(jnp.bfloat16)

        both = jnp.dot(normed[...], kv_w[...], preferred_element_type=jnp.float32)
        keys[...] = turn(both[:, :HEAD], key_gain[...], 1.0)
        values[:, :HEAD] = both[:, HEAD:].astype(jnp.bfloat16)
        values[:, HEAD:] = jnp.ones((SEQ, HEAD), jnp.bfloat16)
        for load in loads[7:9]:
            load.wait()
        factor = math.log2(math.e) / math.sqrt(HEAD)

        def project(n, carry):
            pair = jnp.dot(
                normed[...], query_w[:, rows_at(n, 2 * HEAD)], preferred_element_type=jnp.float32
            )
            for h in range(2):
                head = turn(pair[:, h * HEAD : (h + 1) * HEAD], query_gain[...], factor)
                for i in range(4):
                    queries[i, rows_at(2 * n + h, BLOCK), :] = head[i * BLOCK : (i + 1) * BLOCK]
            return carry

        lax.fori_loop(0, heads // 2, project, 0)
        pl.semaphore_wait(barrier, 10)
        for load in small:
            load.wait()
        for group in range(3):
            axis = AXES[group][0]
            k = block_of(me[axis])
            pltpu.make_async_copy(table_ref, table.at[group, k], p_recv.at[group, k]).start()
            for d in (1, 3, 2):
                push(
                    table_ref,
                    table.at[group, k],
                    p_send.at[group, d],
                    p_recv.at[group, k],
                    moved(me, axis, step(me[axis], d)),
                )
        loads[9].wait()
        def block(index):
            for n in range(heads // 2):
                scores = lax.dot_general(
                    queries[index, n * 2 * BLOCK : (n + 1) * 2 * BLOCK, :],
                    keys[...],
                    (((1,), (1,)), ((), ())),
                    preferred_element_type=jnp.float32,
                )
                mixed = jnp.dot(
                    jnp.exp2(scores).astype(jnp.bfloat16),
                    values[...],
                    preferred_element_type=jnp.float32,
                )
                mixed = (mixed[:, :HEAD] / mixed[:, HEAD:]).astype(jnp.bfloat16)
                for h in range(2):
                    context[:, (2 * n + h) * HEAD : (2 * n + h + 1) * HEAD] = mixed[
                        h * BLOCK : (h + 1) * BLOCK
                    ]

        def part(side):
            return jnp.dot(
                context[...],
                output_w[:, side * half : (side + 1) * half],
                preferred_element_type=jnp.float32,
            )

        block(step(z, 2))
        for side, device in ((0, ahead), (1, behind)):
            leaving[2, side] = part(side).astype(jnp.bfloat16)
            push(
                leaving.at[2, side], halves.at[side], half_send.at[side], half_recv.at[side], device
            )
        for way, (distance, device) in enumerate(((1, ahead), (3, behind))):
            block(step(z, distance))
            for side in (1 - way, way):
                total = part(side)
                if side == way:
                    landed(halves.at[side], half_recv.at[side])
                    total = total + halves[side].astype(jnp.float32)
                leaving[way, side] = total.astype(jnp.bfloat16)
                push(
                    leaving.at[way, side],
                    arrived.at[way, side],
                    full_send.at[way, side],
                    full_recv.at[way, side],
                    device,
                )
        block(z)
        for side in range(2):
            columns = slice(side * half, (side + 1) * half)
            hidden_ref[:, columns] = part(side) + states[rows_at(z, BLOCK), columns].astype(
                jnp.float32
            )
        for d in range(4):
            for group in range(3):
                k = block_of(step(me[AXES[group][0]], d))
                landed(table.at[group, k], p_recv.at[group, k])
                push(
                    table.at[group, k],
                    table.at[group, k],
                    pc_send.at[group, d],
                    p_recv.at[group, k],
                    other,
                )
        for side in range(2):
            columns = slice(side * half, (side + 1) * half)
            for way in range(2):
                landed(arrived.at[way, side], full_recv.at[way, side])
            hidden_ref[:, columns] = hidden_ref[:, columns] + (
                arrived[0, side].astype(jnp.float32) + arrived[1, side].astype(jnp.float32)
            )
        hidden = hidden_ref[...]
        scale = lax.rsqrt(jnp.mean(hidden * hidden, axis=-1, keepdims=True) + EPS)
        rows_ref[...] = (hidden * scale * mixture_gain[...]).astype(jnp.bfloat16)
        for side in range(2):
            landed(halves.at[side], half_send.at[side])
            for way in range(2):
                landed(arrived.at[way, side], full_send.at[way, side])

    bf16 = jnp.bfloat16
    length, width = states_hbm.shape
    span = query_hbm.shape[1]
    inner = gate_hbm.shape[1]
    pl.run_scoped(
        attention,
        pltpu.VMEM((1, width), jnp.float32),
        pltpu.VMEM((1, HEAD), jnp.float32),
        pltpu.VMEM((1, HEAD), jnp.float32),
        pltpu.VMEM((length, HEAD), jnp.float32),
        pltpu.VMEM((length, HEAD), jnp.float32),
        pltpu.VMEM((length, width), bf16),
        pltpu.VMEM((length, width), bf16),
        pltpu.VMEM((width, span), bf16),
        pltpu.VMEM((width, 2 * HEAD), bf16),
        pltpu.VMEM((span, width), bf16),
        pltpu.VMEM((4, span, HEAD), bf16),
        pltpu.VMEM((length, HEAD), bf16),
        pltpu.VMEM((length, 2 * HEAD), bf16),
        pltpu.VMEM((BLOCK, span), bf16),
        pltpu.VMEM((3, 2, BLOCK, width // 2), bf16),
    )

    def chunks_of(part):
        return [(group, 3 * part + group) + CUTS[3 * part + group] for group in range(3)]

    def place_of(group, beta, gamma):
        return (beta, gamma) if group == 1 else (gamma, beta)

    def experts(gate_w, up_w, down_w, *O):
        weights = [
            pltpu.make_async_copy(src, dst, w_sem.at[n])
            for n, (src, dst) in enumerate(
                ((gate_hbm, gate_w), (up_hbm, up_w), (down_hbm, down_w))
            )
        ]

        def gather(part):
            for group, chunk, start, size in chunks_of(part):
                axis = AXES[group][0]
                a = me[axis]
                k = block_of(a)
                mine = rows_ref.at[:, pl.ds(start, size)]
                place = G[chunk].at[rows_at(k, BLOCK)]
                pltpu.make_async_copy(mine, place, g_recv.at[chunk, k]).start()
                for d in (1, 3, 2):
                    push(
                        mine,
                        place,
                        g_send.at[chunk, d],
                        g_recv.at[chunk, k],
                        moved(me, axis, step(a, d)),
                    )

        def across(part):
            for d in (0, 1, 3, 2):
                for group, chunk, start, size in chunks_of(part):
                    k = block_of(step(me[AXES[group][0]], d))
                    place = G[chunk].at[rows_at(k, BLOCK)]
                    landed(place, g_recv.at[chunk, k])
                    push(place, place, gc_send.at[chunk, d], g_recv.at[chunk, k], other)

        def dispatch(*S):
            gather(0)
            for load in weights:
                load.start()
            for group in range(3):
                for a in range(4):
                    k = (1 - core) * 4 + a
                    landed(table.at[group, k], p_recv.at[group, k])
                routes(me, group, False, table, S[group])
            for part in FORTH:
                across(part)
                if part + 1 < len(SETS):
                    gather(part + 1)
                for group, chunk, start, size in chunks_of(part):
                    axis = AXES[group][1]
                    for a in range(4):
                        k = (1 - core) * 4 + a
                        landed(G[chunk].at[rows_at(k, BLOCK)], g_recv.at[chunk, k])

                    def pick(n, carry, group=group, chunk=chunk, axis=axis):
                        mine = me[axis]
                        beta = step(mine, n + 1)
                        O[chunk][beta] = jnp.dot(
                            S[group][rows_at(beta, GROUP), :],
                            G[chunk][...],
                            preferred_element_type=jnp.float32,
                        ).astype(jnp.bfloat16)

                        @pl.when(n < 3)
                        def _():
                            push(
                                O[chunk].at[beta],
                                M[chunk].at[mine],
                                b_send.at[chunk, n],
                                b_recv.at[chunk, mine],
                                moved(me, axis, beta),
                            )

                        @pl.when(n == 3)
                        def _():
                            pltpu.make_async_copy(
                                O[chunk].at[beta], M[chunk].at[mine], b_recv.at[chunk, mine]
                            ).start()

                        return carry

                    lax.fori_loop(0, 4, pick, 0)

        selections = [pltpu.VMEM((4 * GROUP, 8 * BLOCK), bf16) for _ in range(3)]
        pl.run_scoped(dispatch, *selections)

        for part in FORTH:
            for d in (0, 1, 3, 2):
                for group, chunk, start, size in chunks_of(part):
                    _, axis_b, axis_c = AXES[group]
                    beta = step(me[axis_b], d)
                    mine = me[axis_c]
                    landed(M[chunk].at[beta], b_recv.at[chunk, beta])
                    i, j = place_of(group, beta, mine)
                    for e in (1, 3, 2, 0):
                        gamma = step(mine, e)
                        src = M[chunk].at[beta, rows_at(gamma, UNIT)]
                        dst = X[chunk].at[i, rows_at(j, UNIT)]
                        if e:
                            push(
                                src,
                                dst,
                                c_send.at[chunk, d * 4 + e],
                                c_recv.at[chunk, i * 4 + j],
                                moved(me, axis_c, gamma),
                            )
                        else:
                            pltpu.make_async_copy(src, dst, c_recv.at[chunk, i * 4 + j]).start()

        swap = swap_ref[...]

        def apply(gate_sum, up_sum, activated):
            for load in weights:
                load.wait()
            for part in FORTH:
                chunks = chunks_of(part)
                first_chunk, second_chunk, third_chunk = [entry[1] for entry in chunks]
                for group, chunk, start, size in chunks[::-1]:
                    for i in range(4):
                        for j in range(4):
                            landed(
                                X[chunk].at[i, pl.ds(j * UNIT, UNIT)], c_recv.at[chunk, i * 4 + j]
                            )
                for d in range(4):
                    for e in (1, 2, 3):
                        landed(
                            X[third_chunk].at[0, pl.ds(0, UNIT)], c_send.at[third_chunk, d * 4 + e]
                        )

                def regroup(i, carry, chunk=third_chunk):
                    turned = jnp.dot(
                        swap, X[chunk][i], preferred_element_type=jnp.float32
                    ).astype(jnp.bfloat16)
                    for n in range(4):
                        M[chunk][n, rows_at(i, UNIT), :] = turned[n * UNIT : (n + 1) * UNIT]
                    return carry

                lax.fori_loop(0, 4, regroup, 0)

                def project(y, carry, part=part, chunks=chunks):
                    first = X[chunks[0][1]][y]
                    second = jnp.dot(
                        swap, X[chunks[1][1]][y], preferred_element_type=jnp.float32
                    ).astype(jnp.bfloat16)
                    third = M[chunks[2][1]][y]

                    def product(w, before):
                        total = before[y] if part else None
                        for rows, (_, _, start, size) in zip((first, second, third), chunks):
                            term = jnp.dot(
                                rows, w[start : start + size, :], preferred_element_type=jnp.float32
                            )
                            total = term if total is None else total + term
                        return total

                    gate = product(gate_w, gate_sum)
                    up = product(up_w, up_sum)
                    if part + 1 < len(SETS):
                        gate_sum[y] = gate
                        up_sum[y] = up
                    else:
                        gate = gate * gate_scale[...]
                        activated[y] = (
                            gate / (1.0 + jnp.exp(-gate)) * (up * up_scale[...])
                        ).astype(jnp.bfloat16)
                    return carry

                lax.fori_loop(0, 4, project, 0)

            for chunk in range(count):
                for n in range(3):
                    landed(O[chunk].at[0], b_send.at[chunk, n])

            for part in BACK:
                chunks = chunks_of(part)

                def finish(y, entry):
                    _, _, start, size = entry
                    return (
                        jnp.dot(
                            activated[y],
                            down_w[:, start : start + size],
                            preferred_element_type=jnp.float32,
                        )
                        * down_scale[:, start : start + size]
                    ).astype(jnp.bfloat16)

                def lower(n, carry, chunks=chunks):
                    y = step(me["y"], n + 1)
                    chunk = chunks[0][1]
                    O[chunk][y] = finish(y, chunks[0])

                    @pl.when(n < 3)
                    def _():
                        push(
                            O[chunk].at[y],
                            N[chunk].at[me["y"]],
                            rc_send.at[chunk, n],
                            rc_recv.at[chunk, me["y"]],
                            moved(me, "y", y),
                        )

                    @pl.when(n == 3)
                    def _():
                        pltpu.make_async_copy(
                            O[chunk].at[y], N[chunk].at[me["y"]], rc_recv.at[chunk, me["y"]]
                        ).start()

                    next_chunk = chunks[1][1]
                    O[next_chunk][y] = jnp.dot(
                        swap, finish(y, chunks[1]), preferred_element_type=jnp.float32
                    ).astype(jnp.bfloat16)
                    for e in (1, 3, 2, 0):
                        there = step(me["z"], e)
                        src = O[next_chunk].at[y, rows_at(there, UNIT)]
                        dst = N[next_chunk].at[me["z"], rows_at(y, UNIT)]
                        if e:
                            push(
                                src,
                                dst,
                                rc_send.at[next_chunk, n * 4 + e],
                                rc_recv.at[next_chunk, me["z"] * 4 + y],
                                moved(me, "z", there),
                            )
                        else:
                            pltpu.make_async_copy(
                                src, dst, rc_recv.at[next_chunk, me["z"] * 4 + y]
                            ).start()
                    X[chunks[2][1]][y] = finish(y, chunks[2])
                    return carry

                lax.fori_loop(0, 4, lower, 0)

                def restore(n, carry, chunk=chunks[2][1]):
                    mine = me["x"]
                    x = step(mine, n + 1)
                    parts = jnp.concatenate(
                        [X[chunk][y, rows_at(x, UNIT), :] for y in range(4)], axis=0
                    )
                    O[chunk][x] = jnp.dot(
                        swap, parts, preferred_element_type=jnp.float32
                    ).astype(jnp.bfloat16)

                    @pl.when(n < 3)
                    def _():
                        push(
                            O[chunk].at[x],
                            N[chunk].at[mine],
                            rc_send.at[chunk, n],
                            rc_recv.at[chunk, mine],
                            moved(me, "x", x),
                        )

                    @pl.when(n == 3)
                    def _():
                        pltpu.make_async_copy(
                            O[chunk].at[x], N[chunk].at[mine], rc_recv.at[chunk, mine]
                        ).start()

                    return carry

                lax.fori_loop(0, 4, restore, 0)

        pl.run_scoped(
            apply,
            pltpu.VMEM((4, GROUP, inner), jnp.float32),
            pltpu.VMEM((4, GROUP, inner), jnp.float32),
            pltpu.VMEM((4, GROUP, inner), bf16),
        )

        def collect(*S):
            for group in range(3):
                routes(me, group, True, table, S[group])
            for part in BACK:
                for d in (0, 1, 3, 2):
                    for group, chunk, start, size in chunks_of(part):
                        _, axis_b, axis_c = AXES[group]
                        gamma = step(me[axis_c], d)
                        mine = me[axis_b]
                        if group == 1:
                            for n in range(4):
                                landed(
                                    N[chunk].at[gamma, pl.ds(n * UNIT, UNIT)],
                                    rc_recv.at[chunk, gamma * 4 + n],
                                )
                        else:
                            landed(N[chunk].at[gamma], rc_recv.at[chunk, gamma])
                        for e in (1, 3, 2, 0):
                            beta = step(mine, e)
                            src = N[chunk].at[gamma, rows_at(beta, UNIT)]
                            dst = R[chunk].at[rows_at(mine * 4 + gamma, UNIT)]
                            if e:
                                push(
                                    src,
                                    dst,
                                    rb_send.at[chunk, d * 4 + e],
                                    rb_recv.at[chunk, mine * 4 + gamma],
                                    moved(me, axis_b, beta),
                                )
                            else:
                                pltpu.make_async_copy(
                                    src, dst, rb_recv.at[chunk, mine * 4 + gamma]
                                ).start()
            for chunk, (start, size) in enumerate(CUTS):
                for d in (1, 2, 3):
                    landed(rows_ref.at[:, pl.ds(start, size)], g_send.at[chunk, d])
                for d in range(4):
                    landed(G[chunk].at[pl.ds(0, BLOCK)], gc_send.at[chunk, d])

            def total(group, chunk, half):
                return lax.dot_general(
                    S[group][:, rows_at(half, 512)],
                    R[chunk][...],
                    (((0,), (0,)), ((), ())),
                    preferred_element_type=jnp.float32,
                )

            for part in BACK:
                for group, chunk, start, size in chunks_of(part):
                    for j in range(16):
                        landed(R[chunk].at[pl.ds(j * UNIT, UNIT)], rb_recv.at[chunk, j])
                    G[chunk][512:, :] = total(group, chunk, 1 - core).astype(jnp.bfloat16)
                    push(
                        G[chunk].at[pl.ds(512, 512)], H[chunk], k_send.at[chunk], k_recv.at[chunk], other
                    )
                for group, chunk, start, size in chunks_of(part):
                    axis = AXES[group][0]
                    mine = me[axis]
                    own = total(group, chunk, core)
                    landed(H[chunk], k_recv.at[chunk])
                    G[chunk][:512, :] = (own + H[chunk][...].astype(jnp.float32)).astype(
                        jnp.bfloat16
                    )
                    for d in (1, 3, 2):
                        a = step(mine, d)
                        push(
                            G[chunk].at[rows_at(a, BLOCK)],
                            T[chunk].at[d - 1],
                            t_send.at[chunk, d - 1],
                            t_recv.at[chunk, d - 1],
                            moved(me, axis, a),
                        )

        pl.run_scoped(collect, *selections)
        for part in BACK:
            for group, chunk, start, size in chunks_of(part):
                mine = me[AXES[group][0]]
                result = hidden_ref[:, start : start + size] + G[chunk][
                    rows_at(mine, BLOCK), :
                ].astype(jnp.float32)
                for d in range(3):
                    landed(T[chunk].at[d], t_recv.at[chunk, d])
                    result = result + T[chunk][d].astype(jnp.float32)
                out_ref[:, start : start + size] = result.astype(jnp.bfloat16)

        for group in range(3):
            for d in (1, 2, 3):
                landed(table_ref, p_send.at[group, d])
            for d in range(4):
                landed(table_ref, pc_send.at[group, d])
        for part in BACK:
            for group, chunk, start, size in chunks_of(part):
                for n in range(3):
                    if group != 1:
                        landed(O[chunk].at[0], rc_send.at[chunk, n])
                    landed(T[chunk].at[0], t_send.at[chunk, n])
                landed(H[chunk], k_send.at[chunk])
                for d in range(4):
                    for e in (1, 2, 3):
                        unit = R[chunk].at[pl.ds(0, UNIT)]
                        landed(unit, rb_send.at[chunk, d * 4 + e])
                        if group == 1:
                            landed(unit, rc_send.at[chunk, d * 4 + e])
                        if group != 2:
                            landed(unit, c_send.at[chunk, d * 4 + e])

    pl.run_scoped(
        experts,
        pltpu.VMEM((width, inner), bf16),
        pltpu.VMEM((width, inner), bf16),
        pltpu.VMEM((inner, width), bf16),
        *[pltpu.VMEM((4, GROUP, size), bf16) for _, size in CUTS],
    )


def layer(
    states,
    input_gain,
    query_w,
    key_w,
    value_w,
    query_gain,
    key_gain,
    output_w,
    mixture_gain,
    gate_w,
    up_w,
    down_w,
    gate_scale,
    up_scale,
    down_scale,
    table,
):
    length, width = states.shape
    index = np.arange(HEAD // 2, dtype=np.float64)
    angles = np.arange(length, dtype=np.float64)[:, None] * 1e6 ** (-2.0 * index / HEAD)[None, :]
    cosine = np.concatenate([np.cos(angles)] * 2, axis=1).astype(np.float32)
    sine = np.concatenate([-np.sin(angles), np.sin(angles)], axis=1).astype(np.float32)
    line = np.arange(GROUP)
    a, r = line // UNIT, line % UNIT
    source = ((r % 40) // CAP) * UNIT + (r // 40) * 40 + a * CAP + r % CAP
    swap = (source[:, None] == line[None, :]).astype(jnp.bfloat16)
    dma = pltpu.SemaphoreType.DMA
    bf16 = jnp.bfloat16
    count = len(CUTS)
    hbm = pl.BlockSpec(memory_space=pl.ANY)

    def each(shape):
        return [pltpu.VMEM(shape + (size,), bf16) for _, size in CUTS]

    return pl.pallas_call(
        layer_kernel,
        out_shape=jax.ShapeDtypeStruct((BLOCK, width), bf16),
        in_specs=[hbm] * 19,
        out_specs=pl.BlockSpec(memory_space=pltpu.VMEM),
        scratch_shapes=[
            pltpu.VMEM((BLOCK, width), bf16),
            pltpu.VMEM((BLOCK, width), jnp.float32),
            pltpu.VMEM((16, BLOCK), jnp.float32),
            pltpu.VMEM((3, 8, 16, BLOCK), jnp.float32),
            pltpu.VMEM((GROUP, GROUP), bf16),
            pltpu.VMEM(gate_scale.shape, jnp.float32),
            pltpu.VMEM(up_scale.shape, jnp.float32),
            pltpu.VMEM(down_scale.shape, jnp.float32),
            pltpu.VMEM((1, width), jnp.float32),
            pltpu.VMEM((2, BLOCK, width // 2), bf16),
            pltpu.VMEM((2, 2, BLOCK, width // 2), bf16),
            *each((8 * BLOCK,)),
            *each((4, GROUP)),
            *each((4, GROUP)),
            *each((4, GROUP)),
            *each((4 * GROUP,)),
            *each((4 * BLOCK,)),
            *each((3, BLOCK)),
            dma((10,)),
            dma((6,)),
            dma((3,)),
            dma((2,)),
            dma((2,)),
            dma((2, 2)),
            dma((2, 2)),
            dma((3, 4)),
            dma((3, 8)),
            dma((3, 4)),
            dma((count, 4)),
            dma((count, 8)),
            dma((count, 4)),
            dma((count, 4)),
            dma((count, 4)),
            dma((count, 16)),
            dma((count, 16)),
            dma((count, 16)),
            dma((count, 16)),
            dma((count, 16)),
            dma((count, 16)),
            dma((count,)),
            dma((count,)),
            dma((count, 3)),
            dma((count, 3)),
        ],
        compiler_params=pltpu.CompilerParams(
            collective_id=1, has_side_effects=True, vmem_limit_bytes=65000000
        ),
        cost_estimate=pl.CostEstimate(
            flops=31 * 10**9, bytes_accessed=24 * 10**6, transcendentals=4 * 10**6
        ),
        name="layer",
    )(
        states,
        input_gain[None],
        query_gain[None],
        key_gain[None],
        jnp.asarray(cosine),
        jnp.asarray(sine),
        mixture_gain[None],
        query_w,
        key_w,
        value_w,
        output_w,
        table,
        jnp.asarray(swap),
        gate_scale,
        up_scale,
        down_scale,
        gate_w,
        up_w,
        down_w,
    )


def shards(
    states,
    input_gain,
    query_weight,
    key_weight,
    value_weight,
    query_gain,
    key_gain,
    output_weight,
    mixture_gain,
    expert_gate,
    expert_up,
    expert_down,
    gate_scale,
    up_scale,
    down_scale,
    expert_index,
    expert_slot,
    route_weight,
):
    columns = (expert_index[0] * CAP + expert_slot[0]).astype(jnp.float32)
    table = jnp.concatenate([columns.T, route_weight[0].T], axis=0)
    result = layer(
        states[0],
        input_gain,
        query_weight,
        key_weight,
        value_weight,
        query_gain,
        key_gain,
        output_weight,
        mixture_gain,
        expert_gate[0],
        expert_up[0],
        expert_down[0],
        gate_scale,
        up_scale,
        down_scale,
        table,
    )
    return result[None]


def solution(mesh):
    return jax.shard_map(
        shards,
        mesh=mesh,
        in_specs=(
            P(("batch", "ep"), None, None),
            P(),
            P(None, "tp"),
            P(None, "tp"),
            P(None, "tp"),
            P(),
            P(),
            P("tp", None),
            P(),
            P(("batch", "tp", "ep"), None, None),
            P(("batch", "tp", "ep"), None, None),
            P(("batch", "tp", "ep"), None, None),
            P(("batch", "tp", "ep"), None),
            P(("batch", "tp", "ep"), None),
            P(("batch", "tp", "ep"), None),
            P(("batch", "ep"), "tp", None),
            P(("batch", "ep"), "tp", None),
            P(("batch", "ep"), "tp", None),
        ),
        out_specs=P(("batch", "ep"), "tp", None),
        check_vma=False,
    )
```

```python
import math

import jax
import jax.numpy as jnp
import numpy as np
from jax import lax
from jax.experimental import pallas as pl
from jax.experimental.pallas import tpu as pltpu
from jax.sharding import PartitionSpec as P

MESH = pl.DeviceIdType.MESH
SETS = (
    ((0, 512), (768, 384), (1408, 384)),
    ((512, 256), (1152, 256), (1792, 256)),
)
CUTS = tuple(cut for cuts in SETS for cut in cuts)
AXES = (("z", "x", "y"), ("x", "y", "z"), ("y", "z", "x"))
FORTH = tuple(range(len(SETS)))
BACK = FORTH
BLOCK = 128
CAP = 10
UNIT = 8 * CAP
GROUP = 4 * UNIT
EPS = 1e-06
SEQ = 512
HEAD = 128


def position():
    ep = lax.axis_index("ep")
    return {
        "y": lax.axis_index("batch"),
        "z": lax.axis_index("tp"),
        "x": ep // 2,
        "c": ep % 2,
    }


def moved(me, axis, value):
    there = dict(me)
    there[axis] = value
    return (there["y"], there["z"], there["x"] * 2 + there["c"])


def step(value, distance):
    return lax.rem(value + distance, 4)


def rows_at(index, size):
    return pl.ds(pl.multiple_of(index * size, size), size)


def landed(ref, sem):
    pltpu.make_async_copy(ref, ref, sem).wait()


def push(src, dst, send_sem, recv_sem, device):
    pltpu.make_async_remote_copy(
        src_ref=src,
        dst_ref=dst,
        send_sem=send_sem,
        recv_sem=recv_sem,
        device_id=device,
        device_id_type=MESH,
    ).start()


def routes(me, group, weighted, table, select):
    _, axis_b, axis_c = AXES[group]

    def body(j, carry):
        there = dict(me)
        there[axis_b] = j // 4
        there[axis_c] = j % 4
        expert = (there["y"] * 4 + there["z"]) * 8 + there["x"] * 2 + there["c"]
        first = expert.astype(jnp.float32) * CAP
        for k in range(8):
            top = (CAP * k) // 8 * 8
            slot = lax.broadcasted_iota(jnp.int32, (16, BLOCK), 0) + (top - CAP * k)
            wanted = jnp.where(
                (slot >= 0) & (slot < CAP), slot.astype(jnp.float32) + first, -1.0
            )
            found = jnp.zeros((16, BLOCK), jnp.float32)
            for q in range(8):
                column = table[group, k, q : q + 1, :]
                value = table[group, k, 8 + q : 9 + q, :] if weighted else 1.0
                found = jnp.where(wanted == column, value, found)
            parts = [found]
            if top:
                parts.insert(0, jnp.zeros((top, BLOCK), jnp.float32))
            if top < UNIT - 16:
                parts.append(jnp.zeros((UNIT - 16 - top, BLOCK), jnp.float32))
            select[rows_at(j, UNIT), k * BLOCK : (k + 1) * BLOCK] = jnp.concatenate(
                parts, axis=0
            ).astype(jnp.bfloat16)
        return carry

    lax.fori_loop(0, 16, body, 0)


def layer_kernel(*refs):
    (
        states_hbm,
        input_gain_hbm,
        query_gain_hbm,
        key_gain_hbm,
        cosine_hbm,
        sine_hbm,
        mixture_gain_hbm,
        query_hbm,
        key_hbm,
        value_hbm,
        output_hbm,
        expert_hbm,
        slot_hbm,
        route_hbm,
        swap_hbm,
        gate_scale_hbm,
        up_scale_hbm,
        down_scale_hbm,
        gate_hbm,
        up_hbm,
        down_hbm,
        out_ref,
        rows_ref,
        hidden_ref,
        expert_ref,
        slot_ref,
        table_ref,
        table,
        swap_ref,
        gate_scale,
        up_scale,
        down_scale,
        mixture_gain,
        halves,
        arrived,
    ) = refs[:35]
    count = len(CUTS)
    G, M, X, N, R, H, T = [refs[35 + count * i : 35 + count * (i + 1)] for i in range(7)]
    (
        load_sem,
        small_sem,
        w_sem,
        half_send,
        half_recv,
        full_send,
        full_recv,
        p_send,
        p_recv,
        pc_send,
        g_send,
        g_recv,
        gc_send,
        b_send,
        b_recv,
        c_send,
        c_recv,
        rc_send,
        rc_recv,
        rb_send,
        rb_recv,
        k_send,
        k_recv,
        t_send,
        t_recv,
    ) = refs[35 + 7 * count :]
    me = position()
    z = me["z"]
    core = me["c"]
    other = (me["y"], me["z"], me["x"] * 2 + (1 - core))
    ahead = moved(me, "z", step(z, 1))
    behind = moved(me, "z", step(z, 3))

    barrier = pltpu.get_barrier_semaphore()
    for axis in "zxy":
        for d in (1, 2, 3):
            pl.semaphore_signal(
                barrier,
                inc=1,
                device_id=moved(me, axis, step(me[axis], d)),
                device_id_type=MESH,
            )
    pl.semaphore_signal(barrier, inc=1, device_id=other, device_id_type=MESH)

    def block_of(a):
        return core * 4 + a

    def attention(
        input_gain,
        query_gain,
        key_gain,
        cosine,
        sine,
        states,
        normed,
        query_w,
        kv_w,
        output_w,
        queries,
        keys,
        values,
        context,
        leaving,
    ):
        width = states.shape[1]
        half = width // 2
        heads = query_w.shape[1] // HEAD
        loads = [
            pltpu.make_async_copy(src, dst, load_sem.at[n])
            for n, (src, dst) in enumerate(
                (
                    (states_hbm, states),
                    (input_gain_hbm, input_gain),
                    (key_hbm, kv_w.at[:, pl.ds(0, HEAD)]),
                    (value_hbm, kv_w.at[:, pl.ds(HEAD, HEAD)]),
                    (key_gain_hbm, key_gain),
                    (cosine_hbm, cosine),
                    (sine_hbm, sine),
                    (query_gain_hbm, query_gain),
                    (query_hbm, query_w),
                    (output_hbm, output_w),
                )
            )
        ]
        small = [
            pltpu.make_async_copy(src, dst, small_sem.at[n])
            for n, (src, dst) in enumerate(
                (
                    (expert_hbm, expert_ref),
                    (slot_hbm, slot_ref),
                    (route_hbm, table_ref.at[pl.ds(8, 8)]),
                    (mixture_gain_hbm, mixture_gain),
                    (swap_hbm, swap_ref),
                    (gate_scale_hbm, gate_scale),
                    (up_scale_hbm, up_scale),
                    (down_scale_hbm, down_scale),
                )
            )
        ]
        for load in loads + small:
            load.start()
        loads[0].wait()
        loads[1].wait()

        def norm(i, carry):
            part = states[rows_at(i, 128), :].astype(jnp.float32)
            scale = lax.rsqrt(jnp.mean(part * part, axis=-1, keepdims=True) + EPS)
            normed[rows_at(i, 128), :] = (part * scale * input_gain[...]).astype(jnp.bfloat16)
            return carry

        lax.fori_loop(0, SEQ // 128, norm, 0)
        for load in loads[2:7]:
            load.wait()
        def turn(part, gain, factor, cosine, sine):
            scale = lax.rsqrt(jnp.mean(part * part, axis=-1, keepdims=True) + EPS) * factor
            part = part * gain
            return (
                (part * cosine + pltpu.roll(part, HEAD // 2, 1) * sine) * scale
            ).astype(jnp.bfloat16)

        both = jnp.dot(normed[...], kv_w[...], preferred_element_type=jnp.float32)
        keys[...] = turn(both[:, :HEAD], key_gain[...], 1.0, cosine[...], sine[...])
        values[:, :HEAD] = both[:, HEAD:].astype(jnp.bfloat16)
        values[:, HEAD:] = jnp.ones((SEQ, HEAD), jnp.bfloat16)
        for load in loads[7:9]:
            load.wait()
        factor = math.log2(math.e) / math.sqrt(HEAD)

        pl.semaphore_wait(barrier, 10)
        for load in small:
            load.wait()
        table_ref[:8, :] = (expert_ref[...] * CAP + slot_ref[...]).astype(jnp.float32)
        for group in range(3):
            axis = AXES[group][0]
            k = block_of(me[axis])
            pltpu.make_async_copy(table_ref, table.at[group, k], p_recv.at[group, k]).start()
            for d in (1, 3, 2):
                push(
                    table_ref,
                    table.at[group, k],
                    p_send.at[group, d],
                    p_recv.at[group, k],
                    moved(me, axis, step(me[axis], d)),
                )
        loads[9].wait()
        def block(index):
            here = rows_at(index, BLOCK)
            own_cosine = cosine[here, :]
            own_sine = sine[here, :]

            def project(n, carry):
                pair = jnp.dot(
                    normed[here, :],
                    query_w[:, rows_at(n, 2 * HEAD)],
                    preferred_element_type=jnp.float32,
                )
                for h in range(2):
                    queries[rows_at(2 * n + h, BLOCK), :] = turn(
                        pair[:, h * HEAD : (h + 1) * HEAD],
                        query_gain[...],
                        factor,
                        own_cosine,
                        own_sine,
                    )
                return carry

            lax.fori_loop(0, heads // 2, project, 0)
            for n in range(heads // 2):
                scores = lax.dot_general(
                    queries[n * 2 * BLOCK : (n + 1) * 2 * BLOCK, :],
                    keys[...],
                    (((1,), (1,)), ((), ())),
                    preferred_element_type=jnp.float32,
                )
                mixed = jnp.dot(
                    jnp.exp2(scores).astype(jnp.bfloat16),
                    values[...],
                    preferred_element_type=jnp.float32,
                )
                mixed = (mixed[:, :HEAD] / mixed[:, HEAD:]).astype(jnp.bfloat16)
                for h in range(2):
                    context[:, (2 * n + h) * HEAD : (2 * n + h + 1) * HEAD] = mixed[
                        h * BLOCK : (h + 1) * BLOCK
                    ]

        def part(side):
            return jnp.dot(
                context[...],
                output_w[:, side * half : (side + 1) * half],
                preferred_element_type=jnp.float32,
            )

        block(step(z, 2))
        for side, device in ((0, ahead), (1, behind)):
            leaving[2, side] = part(side).astype(jnp.bfloat16)
            push(
                leaving.at[2, side], halves.at[side], half_send.at[side], half_recv.at[side], device
            )
        for way, (distance, device) in enumerate(((1, ahead), (3, behind))):
            block(step(z, distance))
            for side in (1 - way, way):
                total = part(side)
                if side == way:
                    landed(halves.at[side], half_recv.at[side])
                    total = total + halves[side].astype(jnp.float32)
                leaving[way, side] = total.astype(jnp.bfloat16)
                push(
                    leaving.at[way, side],
                    arrived.at[way, side],
                    full_send.at[way, side],
                    full_recv.at[way, side],
                    device,
                )
        block(z)
        for side in range(2):
            columns = slice(side * half, (side + 1) * half)
            hidden_ref[:, columns] = part(side) + states[rows_at(z, BLOCK), columns].astype(
                jnp.float32
            )
        for d in range(4):
            for group in range(3):
                k = block_of(step(me[AXES[group][0]], d))
                landed(table.at[group, k], p_recv.at[group, k])
                push(
                    table.at[group, k],
                    table.at[group, k],
                    pc_send.at[group, d],
                    p_recv.at[group, k],
                    other,
                )
        for side in range(2):
            columns = slice(side * half, (side + 1) * half)
            for way in range(2):
                landed(arrived.at[way, side], full_recv.at[way, side])
            hidden_ref[:, columns] = hidden_ref[:, columns] + (
                arrived[0, side].astype(jnp.float32) + arrived[1, side].astype(jnp.float32)
            )
        hidden = hidden_ref[...]
        scale = lax.rsqrt(jnp.mean(hidden * hidden, axis=-1, keepdims=True) + EPS)
        rows_ref[...] = (hidden * scale * mixture_gain[...]).astype(jnp.bfloat16)
        for side in range(2):
            landed(halves.at[side], half_send.at[side])
            for way in range(2):
                landed(arrived.at[way, side], full_send.at[way, side])

    bf16 = jnp.bfloat16
    length, width = states_hbm.shape
    span = query_hbm.shape[1]
    inner = gate_hbm.shape[1]
    pl.run_scoped(
        attention,
        pltpu.VMEM((1, width), jnp.float32),
        pltpu.VMEM((1, HEAD), jnp.float32),
        pltpu.VMEM((1, HEAD), jnp.float32),
        pltpu.VMEM((length, HEAD), jnp.float32),
        pltpu.VMEM((length, HEAD), jnp.float32),
        pltpu.VMEM((length, width), bf16),
        pltpu.VMEM((length, width), bf16),
        pltpu.VMEM((width, span), bf16),
        pltpu.VMEM((width, 2 * HEAD), bf16),
        pltpu.VMEM((span, width), bf16),
        pltpu.VMEM((span, HEAD), bf16),
        pltpu.VMEM((length, HEAD), bf16),
        pltpu.VMEM((length, 2 * HEAD), bf16),
        pltpu.VMEM((BLOCK, span), bf16),
        pltpu.VMEM((3, 2, BLOCK, width // 2), bf16),
    )

    def chunks_of(part):
        return [(group, 3 * part + group) + CUTS[3 * part + group] for group in range(3)]

    def experts(gate_w, up_w, down_w, *O):
        weights = [
            pltpu.make_async_copy(src, dst, w_sem.at[n])
            for n, (src, dst) in enumerate(
                ((gate_hbm, gate_w), (up_hbm, up_w), (down_hbm, down_w))
            )
        ]

        def gather(part):
            for group, chunk, start, size in chunks_of(part):
                axis = AXES[group][0]
                a = me[axis]
                k = block_of(a)
                mine = rows_ref.at[:, pl.ds(start, size)]
                place = G[chunk].at[rows_at(k, BLOCK)]
                pltpu.make_async_copy(mine, place, g_recv.at[chunk, k]).start()
                for d in (1, 3, 2):
                    push(
                        mine,
                        place,
                        g_send.at[chunk, d],
                        g_recv.at[chunk, k],
                        moved(me, axis, step(a, d)),
                    )

        def across(part):
            for d in (0, 1, 3, 2):
                for group, chunk, start, size in chunks_of(part):
                    k = block_of(step(me[AXES[group][0]], d))
                    place = G[chunk].at[rows_at(k, BLOCK)]
                    landed(place, g_recv.at[chunk, k])
                    push(place, place, gc_send.at[chunk, d], g_recv.at[chunk, k], other)

        def dispatch(*S):
            gather(0)
            for load in weights:
                load.start()
            for group in range(3):
                for a in range(4):
                    k = (1 - core) * 4 + a
                    landed(table.at[group, k], p_recv.at[group, k])
                routes(me, group, False, table, S[group])
            for part in FORTH:
                across(part)
                if part + 1 < len(SETS):
                    gather(part + 1)
                for group, chunk, start, size in chunks_of(part):
                    axis = AXES[group][1]
                    for a in range(4):
                        k = (1 - core) * 4 + a
                        landed(G[chunk].at[rows_at(k, BLOCK)], g_recv.at[chunk, k])

                    def pick(n, carry, group=group, chunk=chunk, axis=axis):
                        mine = me[axis]
                        beta = step(mine, n + 1)
                        O[chunk][beta] = (
                            jnp.dot(
                                S[group][rows_at(beta, GROUP), :],
                                G[chunk][...],
                                preferred_element_type=jnp.float32,
                            )
                            .astype(jnp.bfloat16)
                            .reshape(O[chunk].shape[1:])
                        )

                        @pl.when(n < 3)
                        def _():
                            push(
                                O[chunk].at[beta],
                                M[chunk].at[mine],
                                b_send.at[chunk, n],
                                b_recv.at[chunk, mine],
                                moved(me, axis, beta),
                            )

                        @pl.when(n == 3)
                        def _():
                            pltpu.make_async_copy(
                                O[chunk].at[beta], M[chunk].at[mine], b_recv.at[chunk, mine]
                            ).start()

                        return carry

                    lax.fori_loop(0, 4, pick, 0)

        selections = [pltpu.VMEM((4 * GROUP, 8 * BLOCK), bf16) for _ in range(3)]
        pl.run_scoped(dispatch, *selections)

        def arrival(group, chunk, gamma):
            return X[chunk].at[:, gamma] if group == 1 else X[chunk].at[gamma]

        for part in FORTH:
            for group, chunk, start, size in chunks_of(part):
                axis = AXES[group][2]
                mine = me[axis]
                for beta in range(4):
                    landed(M[chunk].at[beta], b_recv.at[chunk, beta])
                for e in (1, 3, 2, 0):
                    gamma = step(mine, e)
                    src = M[chunk].at[:, gamma]
                    dst = arrival(group, chunk, mine)
                    if e:
                        push(
                            src,
                            dst,
                            c_send.at[chunk, e],
                            c_recv.at[chunk, mine],
                            moved(me, axis, gamma),
                        )
                    else:
                        pltpu.make_async_copy(src, dst, c_recv.at[chunk, mine]).start()

        swap = swap_ref[...]

        def flat(units):
            return units.reshape(-1, units.shape[-1])

        def units_of(rows):
            return rows.reshape(-1, UNIT, rows.shape[-1])

        def apply(gate_sum, up_sum, activated):
            for load in weights:
                load.wait()
            for part in FORTH:
                chunks = chunks_of(part)
                first_chunk, second_chunk, third_chunk = [entry[1] for entry in chunks]
                for group, chunk, start, size in chunks[::-1]:
                    for gamma in range(4):
                        landed(arrival(group, chunk, gamma), c_recv.at[chunk, gamma])
                for e in (1, 2, 3):
                    landed(X[third_chunk].at[0], c_send.at[third_chunk, e])

                def regroup(i, carry, chunk=third_chunk):
                    turned = jnp.dot(
                        swap, flat(X[chunk][i]), preferred_element_type=jnp.float32
                    ).astype(jnp.bfloat16)
                    for n in range(4):
                        M[chunk][n, i] = turned[n * UNIT : (n + 1) * UNIT]
                    return carry

                lax.fori_loop(0, 4, regroup, 0)

                def project(y, carry, part=part, chunks=chunks):
                    first = flat(X[chunks[0][1]][y])
                    second = jnp.dot(
                        swap, flat(X[chunks[1][1]][y]), preferred_element_type=jnp.float32
                    ).astype(jnp.bfloat16)
                    third = flat(M[chunks[2][1]][y])

                    def product(w, before):
                        total = before[y] if part else None
                        for rows, (_, _, start, size) in zip((first, second, third), chunks):
                            term = jnp.dot(
                                rows, w[start : start + size, :], preferred_element_type=jnp.float32
                            )
                            total = term if total is None else total + term
                        return total

                    gate = product(gate_w, gate_sum)
                    up = product(up_w, up_sum)
                    if part + 1 < len(SETS):
                        gate_sum[y] = gate
                        up_sum[y] = up
                    else:
                        gate = gate * gate_scale[...]
                        activated[y] = (
                            gate / (1.0 + jnp.exp(-gate)) * (up * up_scale[...])
                        ).astype(jnp.bfloat16)
                    return carry

                if part + 1 < len(SETS):
                    lax.fori_loop(0, 4, project, 0)

            for chunk in range(count):
                for n in range(3):
                    landed(O[chunk].at[0], b_send.at[chunk, n])

            for part in BACK:
                chunks = chunks_of(part)

                def finish(y, entry):
                    _, _, start, size = entry
                    return (
                        jnp.dot(
                            activated[y],
                            down_w[:, start : start + size],
                            preferred_element_type=jnp.float32,
                        )
                        * down_scale[:, start : start + size]
                    ).astype(jnp.bfloat16)

                def lower(n, carry, part=part, chunks=chunks):
                    y = step(me["y"], n + 1)
                    if part == BACK[0]:
                        project(y, 0)
                    chunk = chunks[0][1]
                    O[chunk][y] = units_of(finish(y, chunks[0]))

                    @pl.when(n < 3)
                    def _():
                        push(
                            O[chunk].at[y],
                            N[chunk].at[me["y"]],
                            rc_send.at[chunk, n],
                            rc_recv.at[chunk, me["y"]],
                            moved(me, "y", y),
                        )

                    @pl.when(n == 3)
                    def _():
                        pltpu.make_async_copy(
                            O[chunk].at[y], N[chunk].at[me["y"]], rc_recv.at[chunk, me["y"]]
                        ).start()

                    next_chunk = chunks[1][1]
                    O[next_chunk][y] = units_of(
                        jnp.dot(
                            swap, finish(y, chunks[1]), preferred_element_type=jnp.float32
                        ).astype(jnp.bfloat16)
                    )
                    for e in (1, 3, 2, 0):
                        there = step(me["z"], e)
                        src = O[next_chunk].at[y, there]
                        dst = N[next_chunk].at[me["z"], y]
                        if e:
                            push(
                                src,
                                dst,
                                rc_send.at[next_chunk, n * 4 + e],
                                rc_recv.at[next_chunk, me["z"] * 4 + y],
                                moved(me, "z", there),
                            )
                        else:
                            pltpu.make_async_copy(
                                src, dst, rc_recv.at[next_chunk, me["z"] * 4 + y]
                            ).start()
                    X[chunks[2][1]][y] = units_of(finish(y, chunks[2]))
                    return carry

                lax.fori_loop(0, 4, lower, 0)

                def restore(n, carry, chunk=chunks[2][1]):
                    mine = me["x"]
                    x = step(mine, n + 1)
                    parts = jnp.concatenate(
                        [X[chunk][y, x] for y in range(4)], axis=0
                    )
                    O[chunk][x] = units_of(
                        jnp.dot(swap, parts, preferred_element_type=jnp.float32).astype(
                            jnp.bfloat16
                        )
                    )

                    @pl.when(n < 3)
                    def _():
                        push(
                            O[chunk].at[x],
                            N[chunk].at[mine],
                            rc_send.at[chunk, n],
                            rc_recv.at[chunk, mine],
                            moved(me, "x", x),
                        )

                    @pl.when(n == 3)
                    def _():
                        pltpu.make_async_copy(
                            O[chunk].at[x], N[chunk].at[mine], rc_recv.at[chunk, mine]
                        ).start()

                    return carry

                lax.fori_loop(0, 4, restore, 0)

        pl.run_scoped(
            apply,
            pltpu.VMEM((4, GROUP, inner), jnp.float32),
            pltpu.VMEM((4, GROUP, inner), jnp.float32),
            pltpu.VMEM((4, GROUP, inner), bf16),
        )

        def collect(select, *W):
            for group in range(3):
                routes(me, group, True, table, select)

                def turn(k, carry, group=group):
                    W[group][rows_at(k, BLOCK), :] = select[:, rows_at(k, BLOCK)].T
                    return carry

                lax.fori_loop(0, 8, turn, 0)
            for part in BACK:
                for group, chunk, start, size in chunks_of(part):
                    axis = AXES[group][1]
                    mine = me[axis]
                    for gamma in range(4):
                        if group == 1:
                            for n in range(4):
                                landed(N[chunk].at[gamma, n], rc_recv.at[chunk, gamma * 4 + n])
                        else:
                            landed(N[chunk].at[gamma], rc_recv.at[chunk, gamma])
                    for e in (1, 3, 2, 0):
                        beta = step(mine, e)
                        src = N[chunk].at[:, beta]
                        dst = R[chunk].at[mine]
                        if e:
                            push(
                                src,
                                dst,
                                rb_send.at[chunk, e],
                                rb_recv.at[chunk, mine],
                                moved(me, axis, beta),
                            )
                        else:
                            pltpu.make_async_copy(src, dst, rb_recv.at[chunk, mine]).start()
            for chunk, (start, size) in enumerate(CUTS):
                for d in (1, 2, 3):
                    landed(rows_ref.at[:, pl.ds(start, size)], g_send.at[chunk, d])
                for d in range(4):
                    landed(G[chunk].at[pl.ds(0, BLOCK)], gc_send.at[chunk, d])

            def total(group, chunk, half):
                return jnp.dot(
                    W[group][rows_at(half, 512), :],
                    flat(R[chunk][...]),
                    preferred_element_type=jnp.float32,
                )

            for part in BACK:
                for group, chunk, start, size in chunks_of(part):
                    for beta in range(4):
                        landed(R[chunk].at[beta], rb_recv.at[chunk, beta])
                    G[chunk][512:, :] = total(group, chunk, 1 - core).astype(jnp.bfloat16)
                    push(
                        G[chunk].at[pl.ds(512, 512)], H[chunk], k_send.at[chunk], k_recv.at[chunk], other
                    )
                for group, chunk, start, size in chunks_of(part):
                    axis = AXES[group][0]
                    mine = me[axis]
                    own = total(group, chunk, core)
                    landed(H[chunk], k_recv.at[chunk])
                    G[chunk][:512, :] = (own + H[chunk][...].astype(jnp.float32)).astype(
                        jnp.bfloat16
                    )
                    for d in (1, 3, 2):
                        a = step(mine, d)
                        push(
                            G[chunk].at[rows_at(a, BLOCK)],
                            T[chunk].at[d - 1],
                            t_send.at[chunk, d - 1],
                            t_recv.at[chunk, d - 1],
                            moved(me, axis, a),
                        )

        pl.run_scoped(
            collect,
            selections[0],
            *[pltpu.VMEM((8 * BLOCK, 4 * GROUP), bf16) for _ in range(3)],
        )
        for part in BACK:
            for group, chunk, start, size in chunks_of(part):
                mine = me[AXES[group][0]]
                result = hidden_ref[:, start : start + size] + G[chunk][
                    rows_at(mine, BLOCK), :
                ].astype(jnp.float32)
                for d in range(3):
                    landed(T[chunk].at[d], t_recv.at[chunk, d])
                    result = result + T[chunk][d].astype(jnp.float32)
                out_ref[:, start : start + size] = result.astype(jnp.bfloat16)

        for group in range(3):
            for d in (1, 2, 3):
                landed(table_ref, p_send.at[group, d])
            for d in range(4):
                landed(table_ref, pc_send.at[group, d])
        for part in BACK:
            for group, chunk, start, size in chunks_of(part):
                for n in range(3):
                    if group != 1:
                        landed(O[chunk].at[0], rc_send.at[chunk, n])
                    landed(T[chunk].at[0], t_send.at[chunk, n])
                landed(H[chunk], k_send.at[chunk])
                for e in (1, 2, 3):
                    landed(R[chunk].at[0], rb_send.at[chunk, e])
                    if group != 2:
                        landed(R[chunk].at[0], c_send.at[chunk, e])
                    if group == 1:
                        for n in range(4):
                            landed(R[chunk].at[0, 0], rc_send.at[chunk, n * 4 + e])

    pl.run_scoped(
        experts,
        pltpu.VMEM((width, inner), bf16),
        pltpu.VMEM((width, inner), bf16),
        pltpu.VMEM((inner, width), bf16),
        *[pltpu.VMEM((4, 4, UNIT, size), bf16) for _, size in CUTS],
    )


def layer(
    states,
    input_gain,
    query_w,
    key_w,
    value_w,
    query_gain,
    key_gain,
    output_w,
    mixture_gain,
    gate_w,
    up_w,
    down_w,
    gate_scale,
    up_scale,
    down_scale,
    expert_index,
    expert_slot,
    route_weight,
):
    length, width = states.shape
    index = np.arange(HEAD // 2, dtype=np.float64)
    angles = np.arange(length, dtype=np.float64)[:, None] * 1e6 ** (-2.0 * index / HEAD)[None, :]
    cosine = np.concatenate([np.cos(angles)] * 2, axis=1).astype(np.float32)
    sine = np.concatenate([-np.sin(angles), np.sin(angles)], axis=1).astype(np.float32)
    line = np.arange(GROUP)
    a, r = line // UNIT, line % UNIT
    source = ((r % 40) // CAP) * UNIT + (r // 40) * 40 + a * CAP + r % CAP
    swap = (source[:, None] == line[None, :]).astype(jnp.bfloat16)
    dma = pltpu.SemaphoreType.DMA
    bf16 = jnp.bfloat16
    count = len(CUTS)
    hbm = pl.BlockSpec(memory_space=pl.ANY)

    def each(shape):
        return [pltpu.VMEM(shape + (size,), bf16) for _, size in CUTS]

    return pl.pallas_call(
        layer_kernel,
        out_shape=jax.ShapeDtypeStruct((BLOCK, width), bf16),
        in_specs=[hbm] * 21,
        out_specs=pl.BlockSpec(memory_space=pltpu.VMEM),
        scratch_shapes=[
            pltpu.VMEM((BLOCK, width), bf16),
            pltpu.VMEM((BLOCK, width), jnp.float32),
            pltpu.VMEM((8, BLOCK), jnp.int32),
            pltpu.VMEM((8, BLOCK), jnp.int32),
            pltpu.VMEM((16, BLOCK), jnp.float32),
            pltpu.VMEM((3, 8, 16, BLOCK), jnp.float32),
            pltpu.VMEM((GROUP, GROUP), bf16),
            pltpu.VMEM(gate_scale.shape, jnp.float32),
            pltpu.VMEM(up_scale.shape, jnp.float32),
            pltpu.VMEM(down_scale.shape, jnp.float32),
            pltpu.VMEM((1, width), jnp.float32),
            pltpu.VMEM((2, BLOCK, width // 2), bf16),
            pltpu.VMEM((2, 2, BLOCK, width // 2), bf16),
            *each((8 * BLOCK,)),
            *each((4, 4, UNIT)),
            *each((4, 4, UNIT)),
            *each((4, 4, UNIT)),
            *each((4, 4, UNIT)),
            *each((4 * BLOCK,)),
            *each((3, BLOCK)),
            dma((10,)),
            dma((8,)),
            dma((3,)),
            dma((2,)),
            dma((2,)),
            dma((2, 2)),
            dma((2, 2)),
            dma((3, 4)),
            dma((3, 8)),
            dma((3, 4)),
            dma((count, 4)),
            dma((count, 8)),
            dma((count, 4)),
            dma((count, 4)),
            dma((count, 4)),
            dma((count, 4)),
            dma((count, 4)),
            dma((count, 16)),
            dma((count, 16)),
            dma((count, 4)),
            dma((count, 4)),
            dma((count,)),
            dma((count,)),
            dma((count, 3)),
            dma((count, 3)),
        ],
        compiler_params=pltpu.CompilerParams(
            collective_id=1, has_side_effects=True, vmem_limit_bytes=65000000
        ),
        cost_estimate=pl.CostEstimate(
            flops=31 * 10**9, bytes_accessed=24 * 10**6, transcendentals=4 * 10**6
        ),
        name="layer",
    )(
        states,
        input_gain[None],
        query_gain[None],
        key_gain[None],
        jnp.asarray(cosine),
        jnp.asarray(sine),
        mixture_gain[None],
        query_w,
        key_w,
        value_w,
        output_w,
        expert_index.T,
        expert_slot.T,
        route_weight.T,
        jnp.asarray(swap),
        gate_scale,
        up_scale,
        down_scale,
        gate_w,
        up_w,
        down_w,
    )


def shards(
    states,
    input_gain,
    query_weight,
    key_weight,
    value_weight,
    query_gain,
    key_gain,
    output_weight,
    mixture_gain,
    expert_gate,
    expert_up,
    expert_down,
    gate_scale,
    up_scale,
    down_scale,
    expert_index,
    expert_slot,
    route_weight,
):
    result = layer(
        states[0],
        input_gain,
        query_weight,
        key_weight,
        value_weight,
        query_gain,
        key_gain,
        output_weight,
        mixture_gain,
        expert_gate[0],
        expert_up[0],
        expert_down[0],
        gate_scale,
        up_scale,
        down_scale,
        expert_index[0],
        expert_slot[0],
        route_weight[0],
    )
    return result[None]


def solution(mesh):
    return jax.shard_map(
        shards,
        mesh=mesh,
        in_specs=(
            P(("batch", "ep"), None, None),
            P(),
            P(None, "tp"),
            P(None, "tp"),
            P(None, "tp"),
            P(),
            P(),
            P("tp", None),
            P(),
            P(("batch", "tp", "ep"), None, None),
            P(("batch", "tp", "ep"), None, None),
            P(("batch", "tp", "ep"), None, None),
            P(("batch", "tp", "ep"), None),
            P(("batch", "tp", "ep"), None),
            P(("batch", "tp", "ep"), None),
            P(("batch", "ep"), "tp", None),
            P(("batch", "ep"), "tp", None),
            P(("batch", "ep"), "tp", None),
        ),
        out_specs=P(("batch", "ep"), "tp", None),
        check_vma=False,
    )
```

```python
import math

import jax
import jax.numpy as jnp
import numpy as np
from jax import lax
from jax.experimental import pallas as pl
from jax.experimental.pallas import tpu as pltpu
from jax.sharding import PartitionSpec as P

MESH = pl.DeviceIdType.MESH
SETS = (
    ((0, 384), (640, 512), (1408, 384)),
    ((384, 256), (1152, 256), (1792, 256)),
)
CUTS = tuple(cut for cuts in SETS for cut in cuts)
AXES = (("z", "x", "y"), ("x", "y", "z"), ("y", "z", "x"))
FORTH = tuple(range(len(SETS)))
BACK = FORTH
BLOCK = 128
CAP = 10
UNIT = 8 * CAP
GROUP = 4 * UNIT
EPS = 1e-06
SEQ = 512
HEAD = 128


def position():
    ep = lax.axis_index("ep")
    return {
        "y": lax.axis_index("batch"),
        "z": lax.axis_index("tp"),
        "x": ep // 2,
        "c": ep % 2,
    }


def moved(me, axis, value):
    there = dict(me)
    there[axis] = value
    return (there["y"], there["z"], there["x"] * 2 + there["c"])


def step(value, distance):
    return lax.rem(value + distance, 4)


def rows_at(index, size):
    return pl.ds(pl.multiple_of(index * size, size), size)


def landed(ref, sem):
    pltpu.make_async_copy(ref, ref, sem).wait()


def push(src, dst, send_sem, recv_sem, device):
    pltpu.make_async_remote_copy(
        src_ref=src,
        dst_ref=dst,
        send_sem=send_sem,
        recv_sem=recv_sem,
        device_id=device,
        device_id_type=MESH,
    ).start()


def routes(me, group, weighted, table, select):
    _, axis_b, axis_c = AXES[group]

    def body(j, carry):
        there = dict(me)
        there[axis_b] = j // 4
        there[axis_c] = j % 4
        expert = (there["y"] * 4 + there["z"]) * 8 + there["x"] * 2 + there["c"]
        first = expert.astype(jnp.float32) * CAP
        for k in range(8):
            top = (CAP * k) // 8 * 8
            slot = lax.broadcasted_iota(jnp.int32, (16, BLOCK), 0) + (top - CAP * k)
            wanted = jnp.where(
                (slot >= 0) & (slot < CAP), slot.astype(jnp.float32) + first, -1.0
            )
            found = jnp.zeros((16, BLOCK), jnp.float32)
            for q in range(8):
                column = table[group, k, q : q + 1, :]
                value = table[group, k, 8 + q : 9 + q, :] if weighted else 1.0
                found = jnp.where(wanted == column, value, found)
            parts = [found]
            if top:
                parts.insert(0, jnp.zeros((top, BLOCK), jnp.float32))
            if top < UNIT - 16:
                parts.append(jnp.zeros((UNIT - 16 - top, BLOCK), jnp.float32))
            select[rows_at(j, UNIT), k * BLOCK : (k + 1) * BLOCK] = jnp.concatenate(
                parts, axis=0
            ).astype(jnp.bfloat16)
        return carry

    lax.fori_loop(0, 16, body, 0)


def layer_kernel(*refs):
    (
        states_hbm,
        input_gain_hbm,
        query_gain_hbm,
        key_gain_hbm,
        cosine_hbm,
        sine_hbm,
        mixture_gain_hbm,
        query_hbm,
        key_hbm,
        value_hbm,
        output_hbm,
        expert_hbm,
        slot_hbm,
        route_hbm,
        swap_hbm,
        gate_scale_hbm,
        up_scale_hbm,
        down_scale_hbm,
        gate_hbm,
        up_hbm,
        down_hbm,
        out_ref,
        rows_ref,
        hidden_ref,
        expert_ref,
        slot_ref,
        table_ref,
        table,
        swap_ref,
        gate_scale,
        up_scale,
        down_scale,
        mixture_gain,
        halves,
        arrived,
    ) = refs[:35]
    count = len(CUTS)
    G, M, X, N, R, H, T = [refs[35 + count * i : 35 + count * (i + 1)] for i in range(7)]
    (
        state_sem,
        load_sem,
        small_sem,
        w_sem,
        half_send,
        half_recv,
        full_send,
        full_recv,
        p_send,
        p_recv,
        pc_send,
        g_send,
        g_recv,
        gc_send,
        b_send,
        b_recv,
        c_send,
        c_recv,
        rc_send,
        rc_recv,
        rb_send,
        rb_recv,
        k_send,
        k_recv,
        t_send,
        t_recv,
    ) = refs[35 + 7 * count :]
    me = position()
    z = me["z"]
    core = me["c"]
    other = (me["y"], me["z"], me["x"] * 2 + (1 - core))
    ahead = moved(me, "z", step(z, 1))
    behind = moved(me, "z", step(z, 3))

    barrier = pltpu.get_barrier_semaphore()
    for axis in "zxy":
        for d in (1, 2, 3):
            pl.semaphore_signal(
                barrier,
                inc=1,
                device_id=moved(me, axis, step(me[axis], d)),
                device_id_type=MESH,
            )
    pl.semaphore_signal(barrier, inc=1, device_id=other, device_id_type=MESH)

    def block_of(a):
        return core * 4 + a

    def attention(
        input_gain,
        query_gain,
        key_gain,
        cosine,
        sine,
        states,
        normed,
        query_w,
        kv_w,
        output_w,
        queries,
        keys,
        values,
        context,
        leaving,
    ):
        width = states.shape[1]
        half = width // 2
        heads = query_w.shape[1] // HEAD
        loads = [
            pltpu.make_async_copy(src, dst, load_sem.at[n])
            for n, (src, dst) in enumerate(
                (
                    (input_gain_hbm, input_gain),
                    (key_hbm, kv_w.at[:, pl.ds(0, HEAD)]),
                    (value_hbm, kv_w.at[:, pl.ds(HEAD, HEAD)]),
                    (key_gain_hbm, key_gain),
                    (cosine_hbm, cosine),
                    (sine_hbm, sine),
                    (query_gain_hbm, query_gain),
                    (query_hbm, query_w),
                    (output_hbm, output_w),
                )
            )
        ]
        small = [
            pltpu.make_async_copy(src, dst, small_sem.at[n])
            for n, (src, dst) in enumerate(
                (
                    (expert_hbm, expert_ref),
                    (slot_hbm, slot_ref),
                    (route_hbm, table_ref.at[pl.ds(8, 8)]),
                    (mixture_gain_hbm, mixture_gain),
                    (swap_hbm, swap_ref),
                    (gate_scale_hbm, gate_scale),
                    (up_scale_hbm, up_scale),
                    (down_scale_hbm, down_scale),
                )
            )
        ]
        quarters = [
            pltpu.make_async_copy(
                states_hbm.at[pl.ds(n * BLOCK, BLOCK)],
                states.at[pl.ds(n * BLOCK, BLOCK)],
                state_sem.at[n],
            )
            for n in range(SEQ // BLOCK)
        ]
        for load in quarters + loads[:7]:
            load.start()
        loads[0].wait()

        def norm(i, carry):
            landed(states.at[rows_at(i, BLOCK)], state_sem.at[i])
            part = states[rows_at(i, 128), :].astype(jnp.float32)
            scale = lax.rsqrt(jnp.mean(part * part, axis=-1, keepdims=True) + EPS)
            normed[rows_at(i, 128), :] = (part * scale * input_gain[...]).astype(jnp.bfloat16)
            return carry

        loads[7].start()
        lax.fori_loop(0, SEQ // 128, norm, 0)
        for load in loads[8:] + small:
            load.start()
        for load in loads[1:6]:
            load.wait()
        def turn(part, gain, factor, cosine, sine):
            scale = lax.rsqrt(jnp.mean(part * part, axis=-1, keepdims=True) + EPS) * factor
            part = part * gain
            return (
                (part * cosine + pltpu.roll(part, HEAD // 2, 1) * sine) * scale
            ).astype(jnp.bfloat16)

        both = jnp.dot(normed[...], kv_w[...], preferred_element_type=jnp.float32)
        keys[...] = turn(both[:, :HEAD], key_gain[...], 1.0, cosine[...], sine[...])
        values[:, :HEAD] = both[:, HEAD:].astype(jnp.bfloat16)
        values[:, HEAD:] = jnp.ones((SEQ, HEAD), jnp.bfloat16)
        for load in loads[6:8]:
            load.wait()
        factor = math.log2(math.e) / math.sqrt(HEAD)

        pl.semaphore_wait(barrier, 10)
        for load in small:
            load.wait()
        table_ref[:8, :] = (expert_ref[...] * CAP + slot_ref[...]).astype(jnp.float32)
        for group in range(3):
            axis = AXES[group][0]
            k = block_of(me[axis])
            pltpu.make_async_copy(table_ref, table.at[group, k], p_recv.at[group, k]).start()
            for d in (1, 3, 2):
                push(
                    table_ref,
                    table.at[group, k],
                    p_send.at[group, d],
                    p_recv.at[group, k],
                    moved(me, axis, step(me[axis], d)),
                )
        loads[8].wait()
        def block(*places):
            here = [rows_at(place, BLOCK) for place in places]
            tall = len(here) * BLOCK

            def stacked(ref):
                return jnp.concatenate([ref[rows, :] for rows in here], axis=0)

            def project(n, carry):
                pair = jnp.dot(
                    stacked(normed),
                    query_w[:, rows_at(n, 2 * HEAD)],
                    preferred_element_type=jnp.float32,
                )
                for h in range(2):
                    queries[rows_at(2 * n + h, tall), :] = turn(
                        pair[:, h * HEAD : (h + 1) * HEAD],
                        query_gain[...],
                        factor,
                        stacked(cosine),
                        stacked(sine),
                    )
                return carry

            lax.fori_loop(0, heads // 2, project, 0)
            joined = 2 * BLOCK // tall
            for n in range(heads // joined):
                scores = lax.dot_general(
                    queries[n * 2 * BLOCK : (n + 1) * 2 * BLOCK, :],
                    keys[...],
                    (((1,), (1,)), ((), ())),
                    preferred_element_type=jnp.float32,
                )
                mixed = jnp.dot(
                    jnp.exp2(scores).astype(jnp.bfloat16),
                    values[...],
                    preferred_element_type=jnp.float32,
                )
                mixed = (mixed[:, :HEAD] / mixed[:, HEAD:]).astype(jnp.bfloat16)
                for h in range(joined):
                    head = joined * n + h
                    context[:tall, head * HEAD : (head + 1) * HEAD] = mixed[
                        h * tall : (h + 1) * tall
                    ]

        def part(side, tall=BLOCK):
            return jnp.dot(
                context[:tall, :],
                output_w[:, side * half : (side + 1) * half],
                preferred_element_type=jnp.float32,
            )

        block(step(z, 2))
        for side, device in ((0, ahead), (1, behind)):
            leaving[2, side] = part(side).astype(jnp.bfloat16)
            push(
                leaving.at[2, side], halves.at[side], half_send.at[side], half_recv.at[side], device
            )

        def leave(way, side, total):
            leaving[way, side] = total.astype(jnp.bfloat16)
            push(
                leaving.at[way, side],
                arrived.at[way, side],
                full_send.at[way, side],
                full_recv.at[way, side],
                (ahead, behind)[way],
            )

        block(step(z, 1), step(z, 3))
        last = part(1, 2 * BLOCK)
        leave(0, 1, last[:BLOCK])
        first = part(0, 2 * BLOCK)
        leave(1, 0, first[BLOCK:])
        landed(halves.at[0], half_recv.at[0])
        leave(0, 0, first[:BLOCK] + halves[0].astype(jnp.float32))
        landed(halves.at[1], half_recv.at[1])
        leave(1, 1, last[BLOCK:] + halves[1].astype(jnp.float32))
        block(z)
        for side in range(2):
            columns = slice(side * half, (side + 1) * half)
            hidden_ref[:, columns] = part(side) + states[rows_at(z, BLOCK), columns].astype(
                jnp.float32
            )
        for d in range(4):
            for group in range(3):
                k = block_of(step(me[AXES[group][0]], d))
                landed(table.at[group, k], p_recv.at[group, k])
                push(
                    table.at[group, k],
                    table.at[group, k],
                    pc_send.at[group, d],
                    p_recv.at[group, k],
                    other,
                )
        for side in range(2):
            columns = slice(side * half, (side + 1) * half)
            for way in range(2):
                landed(arrived.at[way, side], full_recv.at[way, side])
            hidden_ref[:, columns] = hidden_ref[:, columns] + (
                arrived[0, side].astype(jnp.float32) + arrived[1, side].astype(jnp.float32)
            )
        hidden = hidden_ref[...]
        scale = lax.rsqrt(jnp.mean(hidden * hidden, axis=-1, keepdims=True) + EPS)
        rows_ref[...] = (hidden * scale * mixture_gain[...]).astype(jnp.bfloat16)
        for side in range(2):
            landed(halves.at[side], half_send.at[side])
            for way in range(2):
                landed(arrived.at[way, side], full_send.at[way, side])

    bf16 = jnp.bfloat16
    length, width = states_hbm.shape
    span = query_hbm.shape[1]
    inner = gate_hbm.shape[1]
    pl.run_scoped(
        attention,
        pltpu.VMEM((1, width), jnp.float32),
        pltpu.VMEM((1, HEAD), jnp.float32),
        pltpu.VMEM((1, HEAD), jnp.float32),
        pltpu.VMEM((length, HEAD), jnp.float32),
        pltpu.VMEM((length, HEAD), jnp.float32),
        pltpu.VMEM((length, width), bf16),
        pltpu.VMEM((length, width), bf16),
        pltpu.VMEM((width, span), bf16),
        pltpu.VMEM((width, 2 * HEAD), bf16),
        pltpu.VMEM((span, width), bf16),
        pltpu.VMEM((2 * span, HEAD), bf16),
        pltpu.VMEM((length, HEAD), bf16),
        pltpu.VMEM((length, 2 * HEAD), bf16),
        pltpu.VMEM((2 * BLOCK, span), bf16),
        pltpu.VMEM((3, 2, BLOCK, width // 2), bf16),
    )

    def chunks_of(part):
        return [(group, 3 * part + group) + CUTS[3 * part + group] for group in range(3)]

    def experts(gate_w, up_w, down_w, *O):
        weights = [
            pltpu.make_async_copy(src, dst, w_sem.at[n])
            for n, (src, dst) in enumerate(
                ((gate_hbm, gate_w), (up_hbm, up_w), (down_hbm, down_w))
            )
        ]

        def gather(part):
            for group, chunk, start, size in chunks_of(part):
                axis = AXES[group][0]
                a = me[axis]
                k = block_of(a)
                mine = rows_ref.at[:, pl.ds(start, size)]
                place = G[chunk].at[rows_at(k, BLOCK)]
                pltpu.make_async_copy(mine, place, g_recv.at[chunk, k]).start()
                for d in (1, 3, 2):
                    push(
                        mine,
                        place,
                        g_send.at[chunk, d],
                        g_recv.at[chunk, k],
                        moved(me, axis, step(a, d)),
                    )

        def across(part):
            for d in (0, 1, 3, 2):
                for group, chunk, start, size in chunks_of(part):
                    k = block_of(step(me[AXES[group][0]], d))
                    place = G[chunk].at[rows_at(k, BLOCK)]
                    landed(place, g_recv.at[chunk, k])
                    push(place, place, gc_send.at[chunk, d], g_recv.at[chunk, k], other)

        def dispatch(*S):
            gather(0)
            for load in weights:
                load.start()
            for group in range(3):
                for a in range(4):
                    k = (1 - core) * 4 + a
                    landed(table.at[group, k], p_recv.at[group, k])
                routes(me, group, False, table, S[group])
            for part in FORTH:
                across(part)
                if part + 1 < len(SETS):
                    gather(part + 1)
                for group, chunk, start, size in chunks_of(part):
                    axis = AXES[group][1]
                    for a in range(4):
                        k = (1 - core) * 4 + a
                        landed(G[chunk].at[rows_at(k, BLOCK)], g_recv.at[chunk, k])

                    def pick(n, carry, group=group, chunk=chunk, axis=axis):
                        mine = me[axis]
                        beta = step(mine, n + 1)
                        O[chunk][beta] = (
                            jnp.dot(
                                S[group][rows_at(beta, GROUP), :],
                                G[chunk][...],
                                preferred_element_type=jnp.float32,
                            )
                            .astype(jnp.bfloat16)
                            .reshape(O[chunk].shape[1:])
                        )

                        @pl.when(n < 3)
                        def _():
                            push(
                                O[chunk].at[beta],
                                M[chunk].at[mine],
                                b_send.at[chunk, n],
                                b_recv.at[chunk, mine],
                                moved(me, axis, beta),
                            )

                        @pl.when(n == 3)
                        def _():
                            pltpu.make_async_copy(
                                O[chunk].at[beta], M[chunk].at[mine], b_recv.at[chunk, mine]
                            ).start()

                        return carry

                    lax.fori_loop(0, 4, pick, 0)

        selections = [pltpu.VMEM((4 * GROUP, 8 * BLOCK), bf16) for _ in range(3)]
        pl.run_scoped(dispatch, *selections)

        def arrival(group, chunk, gamma):
            return X[chunk].at[:, gamma] if group == 1 else X[chunk].at[gamma]

        for part in FORTH:
            for group, chunk, start, size in chunks_of(part):
                axis = AXES[group][2]
                mine = me[axis]
                for beta in range(4):
                    landed(M[chunk].at[beta], b_recv.at[chunk, beta])
                for e in (1, 3, 2, 0):
                    gamma = step(mine, e)
                    src = M[chunk].at[:, gamma]
                    dst = arrival(group, chunk, mine)
                    if e:
                        push(
                            src,
                            dst,
                            c_send.at[chunk, e],
                            c_recv.at[chunk, mine],
                            moved(me, axis, gamma),
                        )
                    else:
                        pltpu.make_async_copy(src, dst, c_recv.at[chunk, mine]).start()

        swap = swap_ref[...]

        def flat(units):
            return units.reshape(-1, units.shape[-1])

        def units_of(rows):
            return rows.reshape(-1, UNIT, rows.shape[-1])

        def apply(gate_sum, up_sum, activated):
            for load in weights:
                load.wait()
            for part in FORTH:
                chunks = chunks_of(part)
                first_chunk, second_chunk, third_chunk = [entry[1] for entry in chunks]
                for group, chunk, start, size in chunks[::-1]:
                    for gamma in range(4):
                        landed(arrival(group, chunk, gamma), c_recv.at[chunk, gamma])
                for e in (1, 2, 3):
                    landed(X[third_chunk].at[0], c_send.at[third_chunk, e])

                def regroup(i, carry, chunk=third_chunk):
                    turned = jnp.dot(
                        swap, flat(X[chunk][i]), preferred_element_type=jnp.float32
                    ).astype(jnp.bfloat16)
                    for n in range(4):
                        M[chunk][n, i] = turned[n * UNIT : (n + 1) * UNIT]
                    return carry

                lax.fori_loop(0, 4, regroup, 0)

                def project(y, carry, part=part, chunks=chunks):
                    first = flat(X[chunks[0][1]][y])
                    second = jnp.dot(
                        swap, flat(X[chunks[1][1]][y]), preferred_element_type=jnp.float32
                    ).astype(jnp.bfloat16)
                    third = flat(M[chunks[2][1]][y])

                    def product(w, before):
                        total = before[y] if part else None
                        for rows, (_, _, start, size) in zip((first, second, third), chunks):
                            term = jnp.dot(
                                rows, w[start : start + size, :], preferred_element_type=jnp.float32
                            )
                            total = term if total is None else total + term
                        return total

                    gate = product(gate_w, gate_sum)
                    up = product(up_w, up_sum)
                    if part + 1 < len(SETS):
                        gate_sum[y] = gate
                        up_sum[y] = up
                    else:
                        gate = gate * gate_scale[...]
                        activated[y] = (
                            gate / (1.0 + jnp.exp(-gate)) * (up * up_scale[...])
                        ).astype(jnp.bfloat16)
                    return carry

                if part + 1 < len(SETS):
                    lax.fori_loop(0, 4, project, 0)

            for chunk in range(count):
                for n in range(3):
                    landed(O[chunk].at[0], b_send.at[chunk, n])

            for part in BACK:
                chunks = chunks_of(part)

                def finish(y, entry):
                    _, _, start, size = entry
                    return (
                        jnp.dot(
                            activated[y],
                            down_w[:, start : start + size],
                            preferred_element_type=jnp.float32,
                        )
                        * down_scale[:, start : start + size]
                    ).astype(jnp.bfloat16)

                def lower(n, carry, part=part, chunks=chunks):
                    y = step(me["y"], n + 1)
                    if part == BACK[0]:
                        project(y, 0)
                    chunk = chunks[0][1]
                    O[chunk][y] = units_of(finish(y, chunks[0]))

                    @pl.when(n < 3)
                    def _():
                        push(
                            O[chunk].at[y],
                            N[chunk].at[me["y"]],
                            rc_send.at[chunk, n],
                            rc_recv.at[chunk, me["y"]],
                            moved(me, "y", y),
                        )

                    @pl.when(n == 3)
                    def _():
                        pltpu.make_async_copy(
                            O[chunk].at[y], N[chunk].at[me["y"]], rc_recv.at[chunk, me["y"]]
                        ).start()

                    next_chunk = chunks[1][1]
                    O[next_chunk][y] = units_of(
                        jnp.dot(
                            swap, finish(y, chunks[1]), preferred_element_type=jnp.float32
                        ).astype(jnp.bfloat16)
                    )
                    for e in (1, 3, 2, 0):
                        there = step(me["z"], e)
                        src = O[next_chunk].at[y, there]
                        dst = N[next_chunk].at[me["z"], y]
                        if e:
                            push(
                                src,
                                dst,
                                rc_send.at[next_chunk, n * 4 + e],
                                rc_recv.at[next_chunk, me["z"] * 4 + y],
                                moved(me, "z", there),
                            )
                        else:
                            pltpu.make_async_copy(
                                src, dst, rc_recv.at[next_chunk, me["z"] * 4 + y]
                            ).start()
                    X[chunks[2][1]][y] = units_of(finish(y, chunks[2]))
                    return carry

                lax.fori_loop(0, 4, lower, 0)

                def restore(n, carry, chunk=chunks[2][1]):
                    mine = me["x"]
                    x = step(mine, n + 1)
                    parts = jnp.concatenate(
                        [X[chunk][y, x] for y in range(4)], axis=0
                    )
                    O[chunk][x] = units_of(
                        jnp.dot(swap, parts, preferred_element_type=jnp.float32).astype(
                            jnp.bfloat16
                        )
                    )

                    @pl.when(n < 3)
                    def _():
                        push(
                            O[chunk].at[x],
                            N[chunk].at[mine],
                            rc_send.at[chunk, n],
                            rc_recv.at[chunk, mine],
                            moved(me, "x", x),
                        )

                    @pl.when(n == 3)
                    def _():
                        pltpu.make_async_copy(
                            O[chunk].at[x], N[chunk].at[mine], rc_recv.at[chunk, mine]
                        ).start()

                    return carry

                lax.fori_loop(0, 4, restore, 0)

        pl.run_scoped(
            apply,
            pltpu.VMEM((4, GROUP, inner), jnp.float32),
            pltpu.VMEM((4, GROUP, inner), jnp.float32),
            pltpu.VMEM((4, GROUP, inner), bf16),
        )

        def collect(select, *W):
            for group in range(3):
                routes(me, group, True, table, select)

                def turn(k, carry, group=group):
                    W[group][rows_at(k, BLOCK), :] = select[:, rows_at(k, BLOCK)].T
                    return carry

                lax.fori_loop(0, 8, turn, 0)
            for part in BACK:
                for group, chunk, start, size in chunks_of(part):
                    axis = AXES[group][1]
                    mine = me[axis]
                    for gamma in range(4):
                        if group == 1:
                            for n in range(4):
                                landed(N[chunk].at[gamma, n], rc_recv.at[chunk, gamma * 4 + n])
                        else:
                            landed(N[chunk].at[gamma], rc_recv.at[chunk, gamma])
                    for e in (1, 3, 2, 0):
                        beta = step(mine, e)
                        src = N[chunk].at[:, beta]
                        dst = R[chunk].at[mine]
                        if e:
                            push(
                                src,
                                dst,
                                rb_send.at[chunk, e],
                                rb_recv.at[chunk, mine],
                                moved(me, axis, beta),
                            )
                        else:
                            pltpu.make_async_copy(src, dst, rb_recv.at[chunk, mine]).start()
            for chunk, (start, size) in enumerate(CUTS):
                for d in (1, 2, 3):
                    landed(rows_ref.at[:, pl.ds(start, size)], g_send.at[chunk, d])
                for d in range(4):
                    landed(G[chunk].at[pl.ds(0, BLOCK)], gc_send.at[chunk, d])

            def total(group, chunk, half):
                return jnp.dot(
                    W[group][rows_at(half, 512), :],
                    flat(R[chunk][...]),
                    preferred_element_type=jnp.float32,
                )

            for part in BACK:
                for group, chunk, start, size in chunks_of(part):
                    for beta in range(4):
                        landed(R[chunk].at[beta], rb_recv.at[chunk, beta])
                    G[chunk][512:, :] = total(group, chunk, 1 - core).astype(jnp.bfloat16)
                    push(
                        G[chunk].at[pl.ds(512, 512)], H[chunk], k_send.at[chunk], k_recv.at[chunk], other
                    )
                for group, chunk, start, size in chunks_of(part):
                    axis = AXES[group][0]
                    mine = me[axis]
                    own = total(group, chunk, core)
                    landed(H[chunk], k_recv.at[chunk])
                    G[chunk][:512, :] = (own + H[chunk][...].astype(jnp.float32)).astype(
                        jnp.bfloat16
                    )
                    for d in (1, 3, 2):
                        a = step(mine, d)
                        push(
                            G[chunk].at[rows_at(a, BLOCK)],
                            T[chunk].at[d - 1],
                            t_send.at[chunk, d - 1],
                            t_recv.at[chunk, d - 1],
                            moved(me, axis, a),
                        )

        pl.run_scoped(
            collect,
            selections[0],
            *[pltpu.VMEM((8 * BLOCK, 4 * GROUP), bf16) for _ in range(3)],
        )
        for part in BACK:
            for group, chunk, start, size in chunks_of(part):
                mine = me[AXES[group][0]]
                result = hidden_ref[:, start : start + size] + G[chunk][
                    rows_at(mine, BLOCK), :
                ].astype(jnp.float32)
                for d in range(3):
                    landed(T[chunk].at[d], t_recv.at[chunk, d])
                    result = result + T[chunk][d].astype(jnp.float32)
                out_ref[:, start : start + size] = result.astype(jnp.bfloat16)

        for group in range(3):
            for d in (1, 2, 3):
                landed(table_ref, p_send.at[group, d])
            for d in range(4):
                landed(table_ref, pc_send.at[group, d])
        for part in BACK:
            for group, chunk, start, size in chunks_of(part):
                for n in range(3):
                    if group != 1:
                        landed(O[chunk].at[0], rc_send.at[chunk, n])
                    landed(T[chunk].at[0], t_send.at[chunk, n])
                landed(H[chunk], k_send.at[chunk])
                for e in (1, 2, 3):
                    landed(R[chunk].at[0], rb_send.at[chunk, e])
                    if group != 2:
                        landed(R[chunk].at[0], c_send.at[chunk, e])
                    if group == 1:
                        for n in range(4):
                            landed(R[chunk].at[0, 0], rc_send.at[chunk, n * 4 + e])

    pl.run_scoped(
        experts,
        pltpu.VMEM((width, inner), bf16),
        pltpu.VMEM((width, inner), bf16),
        pltpu.VMEM((inner, width), bf16),
        *[pltpu.VMEM((4, 4, UNIT, size), bf16) for _, size in CUTS],
    )


def layer(
    states,
    input_gain,
    query_w,
    key_w,
    value_w,
    query_gain,
    key_gain,
    output_w,
    mixture_gain,
    gate_w,
    up_w,
    down_w,
    gate_scale,
    up_scale,
    down_scale,
    expert_index,
    expert_slot,
    route_weight,
):
    length, width = states.shape
    index = np.arange(HEAD // 2, dtype=np.float64)
    angles = np.arange(length, dtype=np.float64)[:, None] * 1e6 ** (-2.0 * index / HEAD)[None, :]
    cosine = np.concatenate([np.cos(angles)] * 2, axis=1).astype(np.float32)
    sine = np.concatenate([-np.sin(angles), np.sin(angles)], axis=1).astype(np.float32)
    line = np.arange(GROUP)
    a, r = line // UNIT, line % UNIT
    source = ((r % 40) // CAP) * UNIT + (r // 40) * 40 + a * CAP + r % CAP
    swap = (source[:, None] == line[None, :]).astype(jnp.bfloat16)
    dma = pltpu.SemaphoreType.DMA
    bf16 = jnp.bfloat16
    count = len(CUTS)
    hbm = pl.BlockSpec(memory_space=pl.ANY)

    def each(shape):
        return [pltpu.VMEM(shape + (size,), bf16) for _, size in CUTS]

    return pl.pallas_call(
        layer_kernel,
        out_shape=jax.ShapeDtypeStruct((BLOCK, width), bf16),
        in_specs=[hbm] * 21,
        out_specs=pl.BlockSpec(memory_space=pltpu.VMEM),
        scratch_shapes=[
            pltpu.VMEM((BLOCK, width), bf16),
            pltpu.VMEM((BLOCK, width), jnp.float32),
            pltpu.VMEM((8, BLOCK), jnp.int32),
            pltpu.VMEM((8, BLOCK), jnp.int32),
            pltpu.VMEM((16, BLOCK), jnp.float32),
            pltpu.VMEM((3, 8, 16, BLOCK), jnp.float32),
            pltpu.VMEM((GROUP, GROUP), bf16),
            pltpu.VMEM(gate_scale.shape, jnp.float32),
            pltpu.VMEM(up_scale.shape, jnp.float32),
            pltpu.VMEM(down_scale.shape, jnp.float32),
            pltpu.VMEM((1, width), jnp.float32),
            pltpu.VMEM((2, BLOCK, width // 2), bf16),
            pltpu.VMEM((2, 2, BLOCK, width // 2), bf16),
            *each((8 * BLOCK,)),
            *each((4, 4, UNIT)),
            *each((4, 4, UNIT)),
            *each((4, 4, UNIT)),
            *each((4, 4, UNIT)),
            *each((4 * BLOCK,)),
            *each((3, BLOCK)),
            dma((SEQ // BLOCK,)),
            dma((9,)),
            dma((8,)),
            dma((3,)),
            dma((2,)),
            dma((2,)),
            dma((2, 2)),
            dma((2, 2)),
            dma((3, 4)),
            dma((3, 8)),
            dma((3, 4)),
            dma((count, 4)),
            dma((count, 8)),
            dma((count, 4)),
            dma((count, 4)),
            dma((count, 4)),
            dma((count, 4)),
            dma((count, 4)),
            dma((count, 16)),
            dma((count, 16)),
            dma((count, 4)),
            dma((count, 4)),
            dma((count,)),
            dma((count,)),
            dma((count, 3)),
            dma((count, 3)),
        ],
        compiler_params=pltpu.CompilerParams(
            collective_id=1, has_side_effects=True, vmem_limit_bytes=65000000
        ),
        cost_estimate=pl.CostEstimate(
            flops=31 * 10**9, bytes_accessed=24 * 10**6, transcendentals=4 * 10**6
        ),
        name="layer",
    )(
        states,
        input_gain[None],
        query_gain[None],
        key_gain[None],
        jnp.asarray(cosine),
        jnp.asarray(sine),
        mixture_gain[None],
        query_w,
        key_w,
        value_w,
        output_w,
        expert_index.T,
        expert_slot.T,
        route_weight.T,
        jnp.asarray(swap),
        gate_scale,
        up_scale,
        down_scale,
        gate_w,
        up_w,
        down_w,
    )


def shards(
    states,
    input_gain,
    query_weight,
    key_weight,
    value_weight,
    query_gain,
    key_gain,
    output_weight,
    mixture_gain,
    expert_gate,
    expert_up,
    expert_down,
    gate_scale,
    up_scale,
    down_scale,
    expert_index,
    expert_slot,
    route_weight,
):
    result = layer(
        states[0],
        input_gain,
        query_weight,
        key_weight,
        value_weight,
        query_gain,
        key_gain,
        output_weight,
        mixture_gain,
        expert_gate[0],
        expert_up[0],
        expert_down[0],
        gate_scale,
        up_scale,
        down_scale,
        expert_index[0],
        expert_slot[0],
        route_weight[0],
    )
    return result[None]


def solution(mesh):
    return jax.shard_map(
        shards,
        mesh=mesh,
        in_specs=(
            P(("batch", "ep"), None, None),
            P(),
            P(None, "tp"),
            P(None, "tp"),
            P(None, "tp"),
            P(),
            P(),
            P("tp", None),
            P(),
            P(("batch", "tp", "ep"), None, None),
            P(("batch", "tp", "ep"), None, None),
            P(("batch", "tp", "ep"), None, None),
            P(("batch", "tp", "ep"), None),
            P(("batch", "tp", "ep"), None),
            P(("batch", "tp", "ep"), None),
            P(("batch", "ep"), "tp", None),
            P(("batch", "ep"), "tp", None),
            P(("batch", "ep"), "tp", None),
        ),
        out_specs=P(("batch", "ep"), "tp", None),
        check_vma=False,
    )
```

```python
import math

import jax
import jax.numpy as jnp
import numpy as np
from jax import lax
from jax.experimental import pallas as pl
from jax.experimental.pallas import tpu as pltpu
from jax.sharding import PartitionSpec as P

MESH = pl.DeviceIdType.MESH
SETS = (
    ((0, 384), (640, 512), (1408, 384)),
    ((384, 256), (1152, 256), (1792, 256)),
)
CUTS = tuple(cut for cuts in SETS for cut in cuts)
BASES = tuple(sum(size for _, size in CUTS[:n]) for n in range(len(CUTS) + 1))
AXES = (("z", "x", "y"), ("x", "y", "z"), ("y", "z", "x"))
FORTH = tuple(range(len(SETS)))
BACK = FORTH
BLOCK = 128
CAP = 10
UNIT = 8 * CAP
GROUP = 4 * UNIT
EPS = 1e-06
SEQ = 512
HEAD = 128


def position():
    ep = lax.axis_index("ep")
    return {
        "y": lax.axis_index("batch"),
        "z": lax.axis_index("tp"),
        "x": ep // 2,
        "c": ep % 2,
    }


def moved(me, axis, value):
    there = dict(me)
    there[axis] = value
    return (there["y"], there["z"], there["x"] * 2 + there["c"])


def step(value, distance):
    return lax.rem(value + distance, 4)


def rows_at(index, size):
    return pl.ds(pl.multiple_of(index * size, size), size)


def landed(ref, sem):
    pltpu.make_async_copy(ref, ref, sem).wait()


def push(src, dst, send_sem, recv_sem, device):
    pltpu.make_async_remote_copy(
        src_ref=src,
        dst_ref=dst,
        send_sem=send_sem,
        recv_sem=recv_sem,
        device_id=device,
        device_id_type=MESH,
    ).start()


def routes(me, group, weighted, table, select):
    _, axis_b, axis_c = AXES[group]

    def body(j, carry):
        there = dict(me)
        there[axis_b] = j // 4
        there[axis_c] = j % 4
        expert = (there["y"] * 4 + there["z"]) * 8 + there["x"] * 2 + there["c"]
        first = expert.astype(jnp.float32) * CAP
        for k in range(8):
            top = (CAP * k) // 8 * 8
            slot = lax.broadcasted_iota(jnp.int32, (16, BLOCK), 0) + (top - CAP * k)
            wanted = jnp.where(
                (slot >= 0) & (slot < CAP), slot.astype(jnp.float32) + first, -1.0
            )
            found = jnp.zeros((16, BLOCK), jnp.float32)
            for q in range(8):
                column = table[group, k, q : q + 1, :]
                value = table[group, k, 8 + q : 9 + q, :] if weighted else 1.0
                found = jnp.where(wanted == column, value, found)
            parts = [found]
            if top:
                parts.insert(0, jnp.zeros((top, BLOCK), jnp.float32))
            if top < UNIT - 16:
                parts.append(jnp.zeros((UNIT - 16 - top, BLOCK), jnp.float32))
            select[rows_at(j, UNIT), k * BLOCK : (k + 1) * BLOCK] = jnp.concatenate(
                parts, axis=0
            ).astype(jnp.bfloat16)
        return carry

    lax.fori_loop(0, 16, body, 0)


def layer_kernel(*refs):
    (
        states_hbm,
        input_gain_hbm,
        query_gain_hbm,
        key_gain_hbm,
        cosine_hbm,
        sine_hbm,
        mixture_gain_hbm,
        query_hbm,
        key_hbm,
        value_hbm,
        output_hbm,
        expert_hbm,
        slot_hbm,
        route_hbm,
        swap_hbm,
        gate_scale_hbm,
        up_scale_hbm,
        down_scale_hbm,
        gate_hbm,
        up_hbm,
        down_hbm,
        out_ref,
        rows_ref,
        hidden_ref,
        expert_ref,
        slot_ref,
        table_ref,
        table,
        swap_ref,
        gate_scale,
        up_scale,
        down_scale,
        mixture_gain,
        halves,
        arrived,
    ) = refs[:35]
    count = len(CUTS)
    G, M, X, N, R, H, T = [refs[35 + count * i : 35 + count * (i + 1)] for i in range(7)]
    (
        state_sem,
        load_sem,
        small_sem,
        w_sem,
        half_send,
        half_recv,
        full_send,
        full_recv,
        p_send,
        p_recv,
        pc_send,
        g_send,
        g_recv,
        gc_send,
        b_send,
        b_recv,
        c_send,
        c_recv,
        rc_send,
        rc_recv,
        rb_send,
        rb_recv,
        k_send,
        k_recv,
        t_send,
        t_recv,
    ) = refs[35 + 7 * count :]
    me = position()
    z = me["z"]
    core = me["c"]
    other = (me["y"], me["z"], me["x"] * 2 + (1 - core))
    ahead = moved(me, "z", step(z, 1))
    behind = moved(me, "z", step(z, 3))

    barrier = pltpu.get_barrier_semaphore()
    for axis in "zxy":
        for d in (1, 2, 3):
            pl.semaphore_signal(
                barrier,
                inc=1,
                device_id=moved(me, axis, step(me[axis], d)),
                device_id_type=MESH,
            )
    pl.semaphore_signal(barrier, inc=1, device_id=other, device_id_type=MESH)

    def block_of(a):
        return core * 4 + a

    def attention(
        input_gain,
        query_gain,
        key_gain,
        cosine,
        sine,
        states,
        normed,
        query_w,
        kv_w,
        output_w,
        queries,
        keys,
        values,
        context,
        leaving,
    ):
        width = states.shape[1]
        half = width // 2
        heads = query_w.shape[1] // HEAD
        loads = [
            pltpu.make_async_copy(src, dst, load_sem.at[n])
            for n, (src, dst) in enumerate(
                (
                    (input_gain_hbm, input_gain),
                    (key_hbm, kv_w.at[:, pl.ds(0, HEAD)]),
                    (value_hbm, kv_w.at[:, pl.ds(HEAD, HEAD)]),
                    (key_gain_hbm, key_gain),
                    (cosine_hbm, cosine),
                    (sine_hbm, sine),
                    (query_gain_hbm, query_gain),
                    (query_hbm, query_w),
                    (output_hbm, output_w),
                )
            )
        ]
        small = [
            pltpu.make_async_copy(src, dst, small_sem.at[n])
            for n, (src, dst) in enumerate(
                (
                    (expert_hbm, expert_ref),
                    (slot_hbm, slot_ref),
                    (route_hbm, table_ref.at[pl.ds(8, 8)]),
                    (mixture_gain_hbm, mixture_gain),
                    (swap_hbm, swap_ref),
                    (gate_scale_hbm, gate_scale),
                    (up_scale_hbm, up_scale),
                    (down_scale_hbm, down_scale),
                )
            )
        ]
        quarters = [
            pltpu.make_async_copy(
                states_hbm.at[pl.ds(n * BLOCK, BLOCK)],
                states.at[pl.ds(n * BLOCK, BLOCK)],
                state_sem.at[n],
            )
            for n in range(SEQ // BLOCK)
        ]
        for load in quarters + loads[:7]:
            load.start()
        loads[0].wait()

        def norm(i, carry):
            landed(states.at[rows_at(i, BLOCK)], state_sem.at[i])
            part = states[rows_at(i, 128), :].astype(jnp.float32)
            scale = lax.rsqrt(jnp.mean(part * part, axis=-1, keepdims=True) + EPS)
            normed[rows_at(i, 128), :] = (part * scale * input_gain[...]).astype(jnp.bfloat16)
            return carry

        loads[7].start()
        lax.fori_loop(0, SEQ // 128, norm, 0)
        for load in loads[8:] + small:
            load.start()
        for load in loads[1:6]:
            load.wait()
        def turn(part, gain, factor, cosine, sine):
            scale = lax.rsqrt(jnp.mean(part * part, axis=-1, keepdims=True) + EPS) * factor
            part = part * gain
            return (
                (part * cosine + pltpu.roll(part, HEAD // 2, 1) * sine) * scale
            ).astype(jnp.bfloat16)

        both = jnp.dot(normed[...], kv_w[...], preferred_element_type=jnp.float32)
        keys[...] = turn(both[:, :HEAD], key_gain[...], 1.0, cosine[...], sine[...])
        values[:, :HEAD] = both[:, HEAD:].astype(jnp.bfloat16)
        values[:, HEAD:] = jnp.ones((SEQ, HEAD), jnp.bfloat16)
        for load in loads[6:8]:
            load.wait()
        factor = math.log2(math.e) / math.sqrt(HEAD)

        pl.semaphore_wait(barrier, 10)
        for load in small:
            load.wait()
        table_ref[:8, :] = (expert_ref[...] * CAP + slot_ref[...]).astype(jnp.float32)
        for group in range(3):
            axis = AXES[group][0]
            k = block_of(me[axis])
            pltpu.make_async_copy(table_ref, table.at[group, k], p_recv.at[group, k]).start()
            for d in (1, 3, 2):
                push(
                    table_ref,
                    table.at[group, k],
                    p_send.at[group, d],
                    p_recv.at[group, k],
                    moved(me, axis, step(me[axis], d)),
                )
        loads[8].wait()
        def block(*places):
            here = [rows_at(place, BLOCK) for place in places]
            tall = len(here) * BLOCK

            def stacked(ref):
                return jnp.concatenate([ref[rows, :] for rows in here], axis=0)

            def project(n, carry):
                pair = jnp.dot(
                    stacked(normed),
                    query_w[:, rows_at(n, 2 * HEAD)],
                    preferred_element_type=jnp.float32,
                )
                for h in range(2):
                    queries[rows_at(2 * n + h, tall), :] = turn(
                        pair[:, h * HEAD : (h + 1) * HEAD],
                        query_gain[...],
                        factor,
                        stacked(cosine),
                        stacked(sine),
                    )
                return carry

            lax.fori_loop(0, heads // 2, project, 0)
            joined = 2 * BLOCK // tall
            for n in range(heads // joined):
                scores = lax.dot_general(
                    queries[n * 2 * BLOCK : (n + 1) * 2 * BLOCK, :],
                    keys[...],
                    (((1,), (1,)), ((), ())),
                    preferred_element_type=jnp.float32,
                )
                mixed = jnp.dot(
                    jnp.exp2(scores).astype(jnp.bfloat16),
                    values[...],
                    preferred_element_type=jnp.float32,
                )
                mixed = (mixed[:, :HEAD] / mixed[:, HEAD:]).astype(jnp.bfloat16)
                for h in range(joined):
                    head = joined * n + h
                    context[:tall, head * HEAD : (head + 1) * HEAD] = mixed[
                        h * tall : (h + 1) * tall
                    ]

        def part(side, tall=BLOCK):
            return jnp.dot(
                context[:tall, :],
                output_w[:, side * half : (side + 1) * half],
                preferred_element_type=jnp.float32,
            )

        block(step(z, 2))
        for side, device in ((0, ahead), (1, behind)):
            leaving[2, side] = part(side).astype(jnp.bfloat16)
            push(
                leaving.at[2, side], halves.at[side], half_send.at[side], half_recv.at[side], device
            )

        def leave(way, side, total):
            leaving[way, side] = total.astype(jnp.bfloat16)
            push(
                leaving.at[way, side],
                arrived.at[way, side],
                full_send.at[way, side],
                full_recv.at[way, side],
                (ahead, behind)[way],
            )

        block(step(z, 1), step(z, 3))
        last = part(1, 2 * BLOCK)
        leave(0, 1, last[:BLOCK])
        first = part(0, 2 * BLOCK)
        leave(1, 0, first[BLOCK:])
        landed(halves.at[0], half_recv.at[0])
        leave(0, 0, first[:BLOCK] + halves[0].astype(jnp.float32))
        landed(halves.at[1], half_recv.at[1])
        leave(1, 1, last[BLOCK:] + halves[1].astype(jnp.float32))
        block(z)
        for side in range(2):
            columns = slice(side * half, (side + 1) * half)
            hidden_ref[:, columns] = part(side) + states[rows_at(z, BLOCK), columns].astype(
                jnp.float32
            )
        for d in range(4):
            for group in range(3):
                k = block_of(step(me[AXES[group][0]], d))
                landed(table.at[group, k], p_recv.at[group, k])
                push(
                    table.at[group, k],
                    table.at[group, k],
                    pc_send.at[group, d],
                    p_recv.at[group, k],
                    other,
                )
        for side in range(2):
            columns = slice(side * half, (side + 1) * half)
            for way in range(2):
                landed(arrived.at[way, side], full_recv.at[way, side])
            hidden_ref[:, columns] = hidden_ref[:, columns] + (
                arrived[0, side].astype(jnp.float32) + arrived[1, side].astype(jnp.float32)
            )
        hidden = hidden_ref[...]
        scale = lax.rsqrt(jnp.mean(hidden * hidden, axis=-1, keepdims=True) + EPS)
        rows_ref[...] = (hidden * scale * mixture_gain[...]).astype(jnp.bfloat16)
        for side in range(2):
            landed(halves.at[side], half_send.at[side])
            for way in range(2):
                landed(arrived.at[way, side], full_send.at[way, side])

    bf16 = jnp.bfloat16
    length, width = states_hbm.shape
    span = query_hbm.shape[1]
    inner = gate_hbm.shape[1]
    pl.run_scoped(
        attention,
        pltpu.VMEM((1, width), jnp.float32),
        pltpu.VMEM((1, HEAD), jnp.float32),
        pltpu.VMEM((1, HEAD), jnp.float32),
        pltpu.VMEM((length, HEAD), jnp.float32),
        pltpu.VMEM((length, HEAD), jnp.float32),
        pltpu.VMEM((length, width), bf16),
        pltpu.VMEM((length, width), bf16),
        pltpu.VMEM((width, span), bf16),
        pltpu.VMEM((width, 2 * HEAD), bf16),
        pltpu.VMEM((span, width), bf16),
        pltpu.VMEM((2 * span, HEAD), bf16),
        pltpu.VMEM((length, HEAD), bf16),
        pltpu.VMEM((length, 2 * HEAD), bf16),
        pltpu.VMEM((2 * BLOCK, span), bf16),
        pltpu.VMEM((3, 2, BLOCK, width // 2), bf16),
    )

    def chunks_of(part):
        return [(group, 3 * part + group) + CUTS[3 * part + group] for group in range(3)]

    def experts(gate_w, up_w, down_w, *O):
        weights = [
            pltpu.make_async_copy(src, dst, w_sem.at[n])
            for n, (src, dst) in enumerate(
                [(down_hbm, down_w)]
                + [
                    (src.at[pl.ds(start, size)], dst.at[pl.ds(BASES[chunk], size)])
                    for src, dst in ((gate_hbm, gate_w), (up_hbm, up_w))
                    for chunk, (start, size) in enumerate(CUTS)
                ]
            )
        ]

        def gather(part):
            for group, chunk, start, size in chunks_of(part):
                axis = AXES[group][0]
                a = me[axis]
                k = block_of(a)
                mine = rows_ref.at[:, pl.ds(start, size)]
                place = G[chunk].at[rows_at(k, BLOCK)]
                pltpu.make_async_copy(mine, place, g_recv.at[chunk, k]).start()
                for d in (1, 3, 2):
                    push(
                        mine,
                        place,
                        g_send.at[chunk, d],
                        g_recv.at[chunk, k],
                        moved(me, axis, step(a, d)),
                    )

        def across(part):
            for d in (0, 1, 3, 2):
                for group, chunk, start, size in chunks_of(part):
                    k = block_of(step(me[AXES[group][0]], d))
                    place = G[chunk].at[rows_at(k, BLOCK)]
                    landed(place, g_recv.at[chunk, k])
                    push(place, place, gc_send.at[chunk, d], g_recv.at[chunk, k], other)

        def dispatch(*S):
            gather(0)
            for load in weights:
                load.start()
            for group in range(3):
                for a in range(4):
                    k = (1 - core) * 4 + a
                    landed(table.at[group, k], p_recv.at[group, k])
                routes(me, group, False, table, S[group])
            for part in FORTH:
                across(part)
                if part + 1 < len(SETS):
                    gather(part + 1)
                for group, chunk, start, size in chunks_of(part):
                    axis = AXES[group][1]
                    for a in range(4):
                        k = (1 - core) * 4 + a
                        landed(G[chunk].at[rows_at(k, BLOCK)], g_recv.at[chunk, k])

                    def pick(n, carry, group=group, chunk=chunk, axis=axis):
                        mine = me[axis]
                        beta = step(mine, n + 1)
                        O[chunk][beta] = (
                            jnp.dot(
                                S[group][rows_at(beta, GROUP), :],
                                G[chunk][...],
                                preferred_element_type=jnp.float32,
                            )
                            .astype(jnp.bfloat16)
                            .reshape(O[chunk].shape[1:])
                        )

                        @pl.when(n < 3)
                        def _():
                            push(
                                O[chunk].at[beta],
                                M[chunk].at[mine],
                                b_send.at[chunk, n],
                                b_recv.at[chunk, mine],
                                moved(me, axis, beta),
                            )

                        @pl.when(n == 3)
                        def _():
                            pltpu.make_async_copy(
                                O[chunk].at[beta], M[chunk].at[mine], b_recv.at[chunk, mine]
                            ).start()

                        return carry

                    lax.fori_loop(0, 4, pick, 0)

        selections = [pltpu.VMEM((4 * GROUP, 8 * BLOCK), bf16) for _ in range(3)]
        pl.run_scoped(dispatch, *selections)

        def arrival(group, chunk, gamma):
            return X[chunk].at[:, gamma] if group == 1 else X[chunk].at[gamma]

        for part in FORTH:
            for group, chunk, start, size in chunks_of(part):
                axis = AXES[group][2]
                mine = me[axis]
                for beta in range(4):
                    landed(M[chunk].at[beta], b_recv.at[chunk, beta])
                for e in (1, 3, 2, 0):
                    gamma = step(mine, e)
                    src = M[chunk].at[:, gamma]
                    dst = arrival(group, chunk, mine)
                    if e:
                        push(
                            src,
                            dst,
                            c_send.at[chunk, e],
                            c_recv.at[chunk, mine],
                            moved(me, axis, gamma),
                        )
                    else:
                        pltpu.make_async_copy(src, dst, c_recv.at[chunk, mine]).start()

        swap = swap_ref[...]

        def flat(units):
            return units.reshape(-1, units.shape[-1])

        def units_of(rows):
            return rows.reshape(-1, UNIT, rows.shape[-1])

        def apply(gate_sum, up_sum, activated):
            for load in weights:
                load.wait()
            for part in FORTH:
                chunks = chunks_of(part)
                first_chunk, second_chunk, third_chunk = [entry[1] for entry in chunks]
                for group, chunk, start, size in chunks[::-1]:
                    for gamma in range(4):
                        landed(arrival(group, chunk, gamma), c_recv.at[chunk, gamma])
                for e in (1, 2, 3):
                    landed(X[third_chunk].at[0], c_send.at[third_chunk, e])

                def regroup(i, carry, chunk=third_chunk):
                    turned = jnp.dot(
                        swap, flat(X[chunk][i]), preferred_element_type=jnp.float32
                    ).astype(jnp.bfloat16)
                    for n in range(4):
                        M[chunk][n, i] = turned[n * UNIT : (n + 1) * UNIT]
                    return carry

                lax.fori_loop(0, 4, regroup, 0)

                def project(y, carry, part=part, chunks=chunks):
                    first = flat(X[chunks[0][1]][y])
                    second = jnp.dot(
                        swap, flat(X[chunks[1][1]][y]), preferred_element_type=jnp.float32
                    ).astype(jnp.bfloat16)
                    third = flat(M[chunks[2][1]][y])

                    rows = jnp.concatenate([first, second, third], axis=1)

                    def product(w, before):
                        term = jnp.dot(
                            rows,
                            w[BASES[3 * part] : BASES[3 * part + 3], :],
                            preferred_element_type=jnp.float32,
                        )
                        return before[y] + term if part else term

                    gate = product(gate_w, gate_sum)
                    up = product(up_w, up_sum)
                    if part + 1 < len(SETS):
                        gate_sum[y] = gate
                        up_sum[y] = up
                    else:
                        gate = gate * gate_scale[...]
                        activated[y] = (
                            gate / (1.0 + jnp.exp(-gate)) * (up * up_scale[...])
                        ).astype(jnp.bfloat16)
                    return carry

                if part + 1 < len(SETS):
                    lax.fori_loop(0, 4, project, 0)

            for chunk in range(count):
                for n in range(3):
                    landed(O[chunk].at[0], b_send.at[chunk, n])

            for part in BACK:
                chunks = chunks_of(part)

                def finish(y, entry):
                    _, _, start, size = entry
                    return (
                        jnp.dot(
                            activated[y],
                            down_w[:, start : start + size],
                            preferred_element_type=jnp.float32,
                        )
                        * down_scale[:, start : start + size]
                    ).astype(jnp.bfloat16)

                def lower(n, carry, part=part, chunks=chunks):
                    y = step(me["y"], n + 1)
                    if part == BACK[0]:
                        project(y, 0)
                    chunk = chunks[0][1]
                    O[chunk][y] = units_of(finish(y, chunks[0]))

                    @pl.when(n < 3)
                    def _():
                        push(
                            O[chunk].at[y],
                            N[chunk].at[me["y"]],
                            rc_send.at[chunk, n],
                            rc_recv.at[chunk, me["y"]],
                            moved(me, "y", y),
                        )

                    @pl.when(n == 3)
                    def _():
                        pltpu.make_async_copy(
                            O[chunk].at[y], N[chunk].at[me["y"]], rc_recv.at[chunk, me["y"]]
                        ).start()

                    next_chunk = chunks[1][1]
                    O[next_chunk][y] = units_of(
                        jnp.dot(
                            swap, finish(y, chunks[1]), preferred_element_type=jnp.float32
                        ).astype(jnp.bfloat16)
                    )
                    for e in (1, 3, 2, 0):
                        there = step(me["z"], e)
                        src = O[next_chunk].at[y, there]
                        dst = N[next_chunk].at[me["z"], y]
                        if e:
                            push(
                                src,
                                dst,
                                rc_send.at[next_chunk, n * 4 + e],
                                rc_recv.at[next_chunk, me["z"] * 4 + y],
                                moved(me, "z", there),
                            )
                        else:
                            pltpu.make_async_copy(
                                src, dst, rc_recv.at[next_chunk, me["z"] * 4 + y]
                            ).start()
                    X[chunks[2][1]][y] = units_of(finish(y, chunks[2]))
                    return carry

                lax.fori_loop(0, 4, lower, 0)

                def restore(n, carry, chunk=chunks[2][1]):
                    mine = me["x"]
                    x = step(mine, n + 1)
                    parts = jnp.concatenate(
                        [X[chunk][y, x] for y in range(4)], axis=0
                    )
                    O[chunk][x] = units_of(
                        jnp.dot(swap, parts, preferred_element_type=jnp.float32).astype(
                            jnp.bfloat16
                        )
                    )

                    @pl.when(n < 3)
                    def _():
                        push(
                            O[chunk].at[x],
                            N[chunk].at[mine],
                            rc_send.at[chunk, n],
                            rc_recv.at[chunk, mine],
                            moved(me, "x", x),
                        )

                    @pl.when(n == 3)
                    def _():
                        pltpu.make_async_copy(
                            O[chunk].at[x], N[chunk].at[mine], rc_recv.at[chunk, mine]
                        ).start()

                    return carry

                lax.fori_loop(0, 4, restore, 0)

        pl.run_scoped(
            apply,
            pltpu.VMEM((4, GROUP, inner), jnp.float32),
            pltpu.VMEM((4, GROUP, inner), jnp.float32),
            pltpu.VMEM((4, GROUP, inner), bf16),
        )

        def collect(select, *W):
            for group in range(3):
                routes(me, group, True, table, select)

                def turn(k, carry, group=group):
                    W[group][rows_at(k, BLOCK), :] = select[:, rows_at(k, BLOCK)].T
                    return carry

                lax.fori_loop(0, 8, turn, 0)
            for part in BACK:
                for group, chunk, start, size in chunks_of(part):
                    axis = AXES[group][1]
                    mine = me[axis]
                    for gamma in range(4):
                        if group == 1:
                            for n in range(4):
                                landed(N[chunk].at[gamma, n], rc_recv.at[chunk, gamma * 4 + n])
                        else:
                            landed(N[chunk].at[gamma], rc_recv.at[chunk, gamma])
                    for e in (1, 3, 2, 0):
                        beta = step(mine, e)
                        src = N[chunk].at[:, beta]
                        dst = R[chunk].at[mine]
                        if e:
                            push(
                                src,
                                dst,
                                rb_send.at[chunk, e],
                                rb_recv.at[chunk, mine],
                                moved(me, axis, beta),
                            )
                        else:
                            pltpu.make_async_copy(src, dst, rb_recv.at[chunk, mine]).start()
            for chunk, (start, size) in enumerate(CUTS):
                for d in (1, 2, 3):
                    landed(rows_ref.at[:, pl.ds(start, size)], g_send.at[chunk, d])
                for d in range(4):
                    landed(G[chunk].at[pl.ds(0, BLOCK)], gc_send.at[chunk, d])

            def total(group, chunk, half):
                return jnp.dot(
                    W[group][rows_at(half, 512), :],
                    flat(R[chunk][...]),
                    preferred_element_type=jnp.float32,
                )

            for part in BACK:
                for group, chunk, start, size in chunks_of(part):
                    for beta in range(4):
                        landed(R[chunk].at[beta], rb_recv.at[chunk, beta])
                    G[chunk][512:, :] = total(group, chunk, 1 - core).astype(jnp.bfloat16)
                    push(
                        G[chunk].at[pl.ds(512, 512)], H[chunk], k_send.at[chunk], k_recv.at[chunk], other
                    )
                for group, chunk, start, size in chunks_of(part):
                    axis = AXES[group][0]
                    mine = me[axis]
                    own = total(group, chunk, core)
                    landed(H[chunk], k_recv.at[chunk])
                    G[chunk][:512, :] = (own + H[chunk][...].astype(jnp.float32)).astype(
                        jnp.bfloat16
                    )
                    for d in (1, 3, 2):
                        a = step(mine, d)
                        push(
                            G[chunk].at[rows_at(a, BLOCK)],
                            T[chunk].at[d - 1],
                            t_send.at[chunk, d - 1],
                            t_recv.at[chunk, d - 1],
                            moved(me, axis, a),
                        )

        pl.run_scoped(
            collect,
            selections[0],
            *[pltpu.VMEM((8 * BLOCK, 4 * GROUP), bf16) for _ in range(3)],
        )
        for part in BACK:
            for group, chunk, start, size in chunks_of(part):
                mine = me[AXES[group][0]]
                result = hidden_ref[:, start : start + size] + G[chunk][
                    rows_at(mine, BLOCK), :
                ].astype(jnp.float32)
                for d in range(3):
                    landed(T[chunk].at[d], t_recv.at[chunk, d])
                    result = result + T[chunk][d].astype(jnp.float32)
                out_ref[:, start : start + size] = result.astype(jnp.bfloat16)

        for group in range(3):
            for d in (1, 2, 3):
                landed(table_ref, p_send.at[group, d])
            for d in range(4):
                landed(table_ref, pc_send.at[group, d])
        for part in BACK:
            for group, chunk, start, size in chunks_of(part):
                for n in range(3):
                    if group != 1:
                        landed(O[chunk].at[0], rc_send.at[chunk, n])
                    landed(T[chunk].at[0], t_send.at[chunk, n])
                landed(H[chunk], k_send.at[chunk])
                for e in (1, 2, 3):
                    landed(R[chunk].at[0], rb_send.at[chunk, e])
                    if group != 2:
                        landed(R[chunk].at[0], c_send.at[chunk, e])
                    if group == 1:
                        for n in range(4):
                            landed(R[chunk].at[0, 0], rc_send.at[chunk, n * 4 + e])

    pl.run_scoped(
        experts,
        pltpu.VMEM((width, inner), bf16),
        pltpu.VMEM((width, inner), bf16),
        pltpu.VMEM((inner, width), bf16),
        *[pltpu.VMEM((4, 4, UNIT, size), bf16) for _, size in CUTS],
    )


def layer(
    states,
    input_gain,
    query_w,
    key_w,
    value_w,
    query_gain,
    key_gain,
    output_w,
    mixture_gain,
    gate_w,
    up_w,
    down_w,
    gate_scale,
    up_scale,
    down_scale,
    expert_index,
    expert_slot,
    route_weight,
):
    length, width = states.shape
    index = np.arange(HEAD // 2, dtype=np.float64)
    angles = np.arange(length, dtype=np.float64)[:, None] * 1e6 ** (-2.0 * index / HEAD)[None, :]
    cosine = np.concatenate([np.cos(angles)] * 2, axis=1).astype(np.float32)
    sine = np.concatenate([-np.sin(angles), np.sin(angles)], axis=1).astype(np.float32)
    line = np.arange(GROUP)
    a, r = line // UNIT, line % UNIT
    source = ((r % 40) // CAP) * UNIT + (r // 40) * 40 + a * CAP + r % CAP
    swap = (source[:, None] == line[None, :]).astype(jnp.bfloat16)
    dma = pltpu.SemaphoreType.DMA
    bf16 = jnp.bfloat16
    count = len(CUTS)
    hbm = pl.BlockSpec(memory_space=pl.ANY)

    def each(shape):
        return [pltpu.VMEM(shape + (size,), bf16) for _, size in CUTS]

    return pl.pallas_call(
        layer_kernel,
        out_shape=jax.ShapeDtypeStruct((BLOCK, width), bf16),
        in_specs=[hbm] * 21,
        out_specs=pl.BlockSpec(memory_space=pltpu.VMEM),
        scratch_shapes=[
            pltpu.VMEM((BLOCK, width), bf16),
            pltpu.VMEM((BLOCK, width), jnp.float32),
            pltpu.VMEM((8, BLOCK), jnp.int32),
            pltpu.VMEM((8, BLOCK), jnp.int32),
            pltpu.VMEM((16, BLOCK), jnp.float32),
            pltpu.VMEM((3, 8, 16, BLOCK), jnp.float32),
            pltpu.VMEM((GROUP, GROUP), bf16),
            pltpu.VMEM(gate_scale.shape, jnp.float32),
            pltpu.VMEM(up_scale.shape, jnp.float32),
            pltpu.VMEM(down_scale.shape, jnp.float32),
            pltpu.VMEM((1, width), jnp.float32),
            pltpu.VMEM((2, BLOCK, width // 2), bf16),
            pltpu.VMEM((2, 2, BLOCK, width // 2), bf16),
            *each((8 * BLOCK,)),
            *each((4, 4, UNIT)),
            *each((4, 4, UNIT)),
            *each((4, 4, UNIT)),
            *each((4, 4, UNIT)),
            *each((4 * BLOCK,)),
            *each((3, BLOCK)),
            dma((SEQ // BLOCK,)),
            dma((9,)),
            dma((8,)),
            dma((1 + 2 * count,)),
            dma((2,)),
            dma((2,)),
            dma((2, 2)),
            dma((2, 2)),
            dma((3, 4)),
            dma((3, 8)),
            dma((3, 4)),
            dma((count, 4)),
            dma((count, 8)),
            dma((count, 4)),
            dma((count, 4)),
            dma((count, 4)),
            dma((count, 4)),
            dma((count, 4)),
            dma((count, 16)),
            dma((count, 16)),
            dma((count, 4)),
            dma((count, 4)),
            dma((count,)),
            dma((count,)),
            dma((count, 3)),
            dma((count, 3)),
        ],
        compiler_params=pltpu.CompilerParams(
            collective_id=1, has_side_effects=True, vmem_limit_bytes=65000000
        ),
        cost_estimate=pl.CostEstimate(
            flops=31 * 10**9, bytes_accessed=24 * 10**6, transcendentals=4 * 10**6
        ),
        name="layer",
    )(
        states,
        input_gain[None],
        query_gain[None],
        key_gain[None],
        jnp.asarray(cosine),
        jnp.asarray(sine),
        mixture_gain[None],
        query_w,
        key_w,
        value_w,
        output_w,
        expert_index.T,
        expert_slot.T,
        route_weight.T,
        jnp.asarray(swap),
        gate_scale,
        up_scale,
        down_scale,
        gate_w,
        up_w,
        down_w,
    )


def shards(
    states,
    input_gain,
    query_weight,
    key_weight,
    value_weight,
    query_gain,
    key_gain,
    output_weight,
    mixture_gain,
    expert_gate,
    expert_up,
    expert_down,
    gate_scale,
    up_scale,
    down_scale,
    expert_index,
    expert_slot,
    route_weight,
):
    result = layer(
        states[0],
        input_gain,
        query_weight,
        key_weight,
        value_weight,
        query_gain,
        key_gain,
        output_weight,
        mixture_gain,
        expert_gate[0],
        expert_up[0],
        expert_down[0],
        gate_scale,
        up_scale,
        down_scale,
        expert_index[0],
        expert_slot[0],
        route_weight[0],
    )
    return result[None]


def solution(mesh):
    return jax.shard_map(
        shards,
        mesh=mesh,
        in_specs=(
            P(("batch", "ep"), None, None),
            P(),
            P(None, "tp"),
            P(None, "tp"),
            P(None, "tp"),
            P(),
            P(),
            P("tp", None),
            P(),
            P(("batch", "tp", "ep"), None, None),
            P(("batch", "tp", "ep"), None, None),
            P(("batch", "tp", "ep"), None, None),
            P(("batch", "tp", "ep"), None),
            P(("batch", "tp", "ep"), None),
            P(("batch", "tp", "ep"), None),
            P(("batch", "ep"), "tp", None),
            P(("batch", "ep"), "tp", None),
            P(("batch", "ep"), "tp", None),
        ),
        out_specs=P(("batch", "ep"), "tp", None),
        check_vma=False,
    )
```
